32 devices in a mesh: req: 4 (over x, core), seq: 8 (over z, y).
Axes of the slice: x: 2, y: 2, z: 4, core: 2. Of those that a mesh axis runs over, the one named last changes fastest.
Arguments:
- conv_input: bfloat16 [4, 4096, 5120], P('req', 'seq'), may hold values from -6 to 6
- gate_projected: bfloat16 [4, 4096, 4096], P('req', 'seq'), may hold values from -6 to 6
- step_raw: float32 [4, 4096, 64], P('req', 'seq'), may hold values from -1.5 to 6.5
- step_bias: float32 [64], replicated, may hold values from -16 to -3
- decay_log: float32 [64], replicated, may hold values from -0.35 to 0.35
- head_direct_gain: float32 [64], replicated, may hold values from 0.2 to 1
- conv_weight: float32 [4, 5120], replicated, may hold values from -3 to 3
- convolution_bias: float32 [5120], replicated, may hold values from -0.5 to 0.5
- norm_weight: float32 [4096], replicated, may hold values from 0.5 to 1.5
- lengths: int32 [4, 4], P('req'), may hold values from 1 to 2048, 4096 in all within a row
- out_weight: bfloat16 [4096, 4096], P(('req', 'seq')), may hold values from -0.1875 to 0.1875
- residual_last: bfloat16 [4, 4, 4096], replicated, may hold values from -6 to 6
- final_gain: float32 [4096], replicated, may hold values from 0.5 to 1.5
- vocab_weight: bfloat16 [131072, 4096], P(('req', 'seq')), may hold values from -0.25 to 0.25
Outputs:
- y_gated: bfloat16 [4, 4096, 4096], P('req', 'seq')
- final_states: float32 [4, 4, 64, 64, 128], P('req', None, 'seq')
- last_hidden: bfloat16 [4, 4, 4096], P('req')
- max_logit: float32 [4, 4], P('req')
The draws below stay inside these ranges and needn't reach their ends.
Inputs may be any that keep to these rules, and one draw needn't show every extreme that they name: The 4 lengths of a row sum to 4096.
All inputs are finite; a program needn't handle non-finite values.
Results may differ from the reference program's by a relative error of at most 0.0046.
Values may be sent and summed in bfloat16 or wider, within the bound.
No kernel may reach another device: no remote copies, remote signals or barrier semaphores. Data moves between devices by JAX's collectives and lax.ppermute only.
A program may use at most 256 MiB of HBM per device.

```python
import math
import jax
import jax.numpy as jnp
import numpy as np
from jax import lax

D = 4096
HEADS = 64
CHANNEL_WIDTH = 64
GROUPS = 4
STATE = 128
KERNEL = 4
BLOCK = 256
VOCAB = 131072
SEQS = 4
INNER = 4096
CONV = 5120
ROWS = 4
LEN = 4096


def draw_step_bias(key, part):
    first_key, second_key, third_key = jax.random.split(key, 3)
    share = 0.5
    quick = jax.random.uniform(first_key, (HEADS,)) < share
    fast = 1.0 / 40.0 * jnp.exp(jax.random.uniform(second_key, (HEADS,), minval=-0.3, maxval=0.3))
    slow = jnp.exp(jax.random.uniform(third_key, (HEADS,), minval=-0.7, maxval=0.2)) / LEN
    rate = jnp.where(quick, fast, slow)
    return jnp.log(jnp.expm1(rate)).astype(jnp.float32)


def draw_step_raw(key, part):
    first_key, second_key = jax.random.split(key, 2)
    gaussian_jitter = jnp.clip(0.3 * jax.random.normal(first_key, (ROWS, LEN, HEADS)), -1.5, 1.5)
    opening_offsets = jax.random.randint(second_key, (ROWS, 3), 0, LEN)
    run_length = max(LEN // 256, 1)
    places = jnp.arange(LEN)
    within_tile = (places[None, None, :] >= opening_offsets[:, :, None]) & (places[None, None, :] < opening_offsets[:, :, None] + run_length)
    packed_stretch = jnp.any(within_tile, axis=1).astype(jnp.float32)
    return (gaussian_jitter + 5.0 * packed_stretch[:, :, None]).astype(jnp.float32)


def raised(drawn, rng, source, target, parts, factor):
    def block_of(position):
        return (jnp.arange(drawn.shape[position]) // (drawn.shape[position] // parts)).reshape((-1,) + (1,) * (drawn.ndim - 1 - position))

    near = jax.random.permutation(rng, parts)[block_of(target)]
    other_side = (block_of(target) + parts // 2) % parts
    return jnp.where((block_of(source) == near) | (block_of(source) == other_side), factor * drawn, drawn)


def steps_of(stream_key, shape, cuts, low, high):
    def one(axis_at, shards_of):
        heights = jax.random.uniform(jax.random.fold_in(jax.random.fold_in(stream_key, 6), axis_at), (shards_of,), jnp.float32, low / len(cuts), high / len(cuts))
        return jnp.repeat(jnp.exp(heights), shape[axis_at] // shards_of).reshape((-1,) + (1,) * (len(shape) - axis_at - 1))

    loudness = one(*cuts[0])
    for cut in cuts[1:]:
        loudness = loudness * one(*cut)
    return loudness


def length_profile(amount, total, most, skew):
    weights = [(1 << 20) // math.isqrt(standing ** skew) + 1 for standing in range(2, amount + 1)]
    rest, holding = total - most - (amount - 1), [1] * (amount - 1)
    while rest > 0:
        candidates = [i for i in range(amount - 1) if holding[i] < most]
        mass, remaining = sum([weights[i] for i in candidates]), rest
        for i in candidates:
            addition = min(most - holding[i], max(1, remaining * weights[i] // mass), rest)
            holding[i] = holding[i] + addition
            rest = rest - addition
    return np.array([most] + holding)


def uneven_parts(stream_key, number_of, total, limit, lean):
    if number_of == 2:
        one = jax.random.randint(stream_key, (), max(1, total - limit), min(limit, total - 1) + 1)
        return jnp.stack([one, total - one])
    sizes = jnp.asarray(length_profile(number_of, total, limit, lean), jnp.int32)
    twos = (number_of - 1) // 2
    giver, sink = sizes[1:1 + 2 * twos:2], sizes[2:2 + 2 * twos:2]
    slack = jnp.minimum(giver - 1, limit - sink)
    shifted = jax.random.randint(jax.random.fold_in(stream_key, 1), (twos,), 0, 1 << 20) % (slack + 1)
    sizes = sizes.at[1:1 + 2 * twos:2].set(giver - shifted).at[2:2 + 2 * twos:2].set(sink + shifted)
    return sizes[jax.random.permutation(jax.random.fold_in(stream_key, 2), number_of)]


def bell_draw(key, extent, scale, bound, cuts=(), kind=jnp.bfloat16):
    result = jax.random.normal(key, extent, jnp.float32) * scale
    if len(cuts) > 0:
        result = steps_of(key, extent, cuts, -0.22, 0.18) * result
    return jnp.clip(result, min=-bound, max=bound).astype(kind)


def heavy_noise(own_key, dims, scale, bound, cuts, heavy, held_as=jnp.bfloat16):
    result = scale * jax.random.normal(own_key, dims, jnp.float32)
    if cuts:
        result = result * steps_of(own_key, dims, cuts, -0.22, 0.18)
    return jnp.clip(raised(result, jax.random.fold_in(own_key, 3), *heavy), -bound, bound).astype(held_as)


def setup_inputs(seed: int = 0) -> dict:
    seeds = jax.random.split(jax.random.key(seed), 15)
    conv_input = bell_draw(seeds[0], (ROWS, LEN, CONV), 1.0, 6.0, ((0, 4), (1, 8)))
    gate_projected = bell_draw(seeds[1], (ROWS, LEN, INNER), 1.0, 6.0, ((0, 4), (1, 8)))
    step_raw = draw_step_raw(jax.random.fold_in(seeds[14], 71), 0)
    step_bias = draw_step_bias(jax.random.fold_in(seeds[14], 71), 0)
    decay_log = jnp.clip(jax.random.uniform(seeds[4], (HEADS,), jnp.float32, -0.35, 0.35), -0.35, 0.35)
    head_direct_gain = jnp.clip(jax.random.uniform(seeds[5], (HEADS,), jnp.float32, 0.2, 1.0), 0.2, 1.0)
    conv_weight = bell_draw(seeds[6], (KERNEL, CONV), KERNEL ** -0.5, 3.0, (), jnp.float32)
    convolution_bias = jnp.clip(jax.random.uniform(seeds[7], (CONV,), jnp.float32, -0.5, 0.5), -0.5, 0.5)
    norm_weight = jnp.clip(1.0 + 0.1 * jax.random.normal(seeds[8], (INNER,), jnp.float32), 0.5, 1.5)
    lengths = jax.vmap(lambda own: uneven_parts(own, SEQS, LEN, LEN // 2, 2))(jax.random.split(seeds[9], ROWS)).reshape((ROWS, SEQS)).astype(jnp.int32)
    out_weight = heavy_noise(seeds[10], (INNER, D), INNER ** -0.5, 0.1875, ((0, 32),), (0, 1, 32, 2.75))
    residual_last = bell_draw(seeds[11], (ROWS, SEQS, D), 1.0, 6.0)
    final_gain = jnp.clip(1.0 + 0.1 * jax.random.normal(seeds[12], (D,), jnp.float32), 0.5, 1.5)
    vocab_weight = bell_draw(seeds[13], (VOCAB, D), (D // 9) ** -0.5, 0.25, ((0, 32),))
    return dict(conv_input=conv_input, gate_projected=gate_projected, step_raw=step_raw, step_bias=step_bias, decay_log=decay_log, head_direct_gain=head_direct_gain, conv_weight=conv_weight, convolution_bias=convolution_bias, norm_weight=norm_weight, lengths=lengths, out_weight=out_weight, residual_last=residual_last, final_gain=final_gain, vocab_weight=vocab_weight)


TINY_FLOOR = 1e-05

def segment_of(places, lengths):
    bounds = jnp.cumsum(lengths).astype(jnp.int32)[:-1]
    return lax.optimization_barrier(jnp.sum((places[:, None] >= bounds[None, :]).astype(jnp.int32), axis=1)).astype(jnp.int32)

def convolve(padded, padded_seg, conv_weight, convolution_bias, count):
    target = padded_seg[KERNEL - 1:]
    total = jnp.zeros((count, padded.shape[1]), jnp.float32) + convolution_bias
    for kernel_tap in range(KERNEL):
        same_seg = (padded_seg[kernel_tap:kernel_tap + count] == target).astype(jnp.float32)
        total = total + conv_weight[kernel_tap] * padded[kernel_tap:kernel_tap + count].astype(jnp.float32) * same_seg[:, None]
    return jax.nn.silu(total)

def block_parts(feature_matrix, state_inputs, input_map, state_map, output_map, step_size, decays, segment, before):
    length = feature_matrix.shape[0]
    per_group = HEADS // GROUPS
    cum_decay = jnp.cumsum(decays, axis=0)
    places = jnp.arange(length)
    allowed = (places[:, None] >= places[None, :]) & (segment[:, None] == segment[None, :])
    spread = cum_decay.T[:, :, None] - cum_decay.T[:, None, :]
    weights = jnp.exp(jnp.where(allowed[None], spread, -jnp.inf)) * step_size.T[:, None, :]
    scores = jnp.einsum('tgn,sgn->gts', output_map.astype(jnp.float32), input_map.astype(jnp.float32))
    mixing = (weights.reshape(GROUPS, per_group, length, length) * scores[:, None]).astype(jnp.bfloat16)
    grouped = feature_matrix.reshape(length, GROUPS, per_group, CHANNEL_WIDTH)
    y_intra = jnp.einsum('gjts,sgjp->tgjp', mixing.astype(jnp.float32), grouped.astype(jnp.float32)).reshape(length, HEADS, CHANNEL_WIDTH)
    tail_seg = (segment == segment[length - 1]).astype(jnp.float32)
    tail_weight = jnp.exp(cum_decay[length - 1][None, :] - cum_decay) * step_size * tail_seg[:, None]
    scaled = state_inputs * tail_weight[:, :, None]
    state = jnp.einsum('sgjp,sgn->gjpn', scaled.reshape(length, GROUPS, per_group, CHANNEL_WIDTH), state_map, precision=lax.Precision.HIGHEST).reshape(HEADS, CHANNEL_WIDTH, STATE)
    within_tile = (segment == before).astype(jnp.float32)
    lead = jnp.exp(cum_decay) * within_tile[:, None]
    carry = jnp.exp(cum_decay[length - 1]) * within_tile[length - 1]
    return (y_intra, lead, state, carry)

def block_output(y_intra, lead, entering, output_map, feature_matrix, head_direct_gain):
    length = feature_matrix.shape[0]
    per_group = HEADS // GROUPS
    inter = jnp.einsum('tgn,gjpn->tgjp', output_map.astype(jnp.float32), entering.reshape(GROUPS, per_group, CHANNEL_WIDTH, STATE), precision=lax.Precision.HIGHEST).reshape(length, HEADS, CHANNEL_WIDTH)
    return y_intra + lead[:, :, None] * inter + head_direct_gain[None, :, None] * feature_matrix.astype(jnp.float32)

def gate_norm(values, gate, norm_weight):
    length = values.shape[0]
    flat = values.reshape(length, -1) * jax.nn.silu(gate.astype(jnp.float32))
    grouped = flat.reshape(length, GROUPS, -1)
    scale = lax.rsqrt(lax.optimization_barrier(jnp.mean(grouped * grouped, axis=-1, keepdims=True)) + TINY_FLOOR)
    return ((grouped * scale).reshape(length, -1) * norm_weight).astype(jnp.bfloat16)

def state_at(state_inputs, state_map, step_size, decays, segment, before, within, entering):
    length = state_inputs.shape[0]
    per_group = HEADS // GROUPS
    cum_decay = jnp.cumsum(decays, axis=0)
    places = jnp.arange(length)
    allowed = (segment == segment[within]) & (places <= within)
    tail_weight = jnp.exp(jnp.where(allowed[:, None], cum_decay[within][None, :] - cum_decay, -jnp.inf)) * step_size
    scaled = state_inputs * tail_weight[:, :, None]
    state = jnp.einsum('sgjp,sgn->gjpn', scaled.reshape(length, GROUPS, per_group, CHANNEL_WIDTH), state_map, precision=lax.Precision.HIGHEST).reshape(HEADS, CHANNEL_WIDTH, STATE)
    lead = jnp.exp(cum_decay[within]) * (segment[within] == before).astype(jnp.float32)
    return lead[:, None, None] * entering + state

def reference(conv_input, gate_projected, step_raw, step_bias, decay_log, head_direct_gain, conv_weight, convolution_bias, norm_weight, lengths, out_weight, residual_last, final_gain, vocab_weight):
    total_len = conv_input.shape[1]
    inner = HEADS * CHANNEL_WIDTH
    count = total_len // BLOCK
    split_at = inner + GROUPS * STATE

    def one_row(items):
        conv_row, gate_row, raw_row, length_row = items
        places = jnp.arange(total_len, dtype=jnp.int32)
        segment = segment_of(places, length_row)
        padded = jnp.concatenate([jnp.zeros((KERNEL - 1, conv_row.shape[1]), jnp.bfloat16), conv_row], axis=0)
        padded_seg = jnp.concatenate([jnp.full((KERNEL - 1,), -1, jnp.int32), segment], axis=0)
        mixed_full = convolve(padded, padded_seg, conv_weight, convolution_bias, total_len)
        mixed = mixed_full.astype(jnp.bfloat16)
        feature_matrix = mixed[:, :inner].reshape(total_len, HEADS, CHANNEL_WIDTH)
        input_map = mixed[:, inner:split_at].reshape(total_len, GROUPS, STATE)
        output_map = mixed[:, split_at:].reshape(total_len, GROUPS, STATE)
        state_inputs = mixed_full[:, :inner].reshape(total_len, HEADS, CHANNEL_WIDTH)
        state_map = mixed_full[:, inner:split_at].reshape(total_len, GROUPS, STATE)
        step_size = jax.nn.softplus(raw_row + step_bias)
        decays = -jnp.exp(decay_log) * step_size
        befores = segment_of(jnp.arange(count, dtype=jnp.int32) * BLOCK - 1, length_row)
        blocks = (feature_matrix.reshape(count, BLOCK, HEADS, CHANNEL_WIDTH), state_inputs.reshape(count, BLOCK, HEADS, CHANNEL_WIDTH), input_map.reshape(count, BLOCK, GROUPS, STATE), state_map.reshape(count, BLOCK, GROUPS, STATE), output_map.reshape(count, BLOCK, GROUPS, STATE), step_size.reshape(count, BLOCK, HEADS), decays.reshape(count, BLOCK, HEADS), segment.reshape(count, BLOCK), befores, gate_row.reshape(count, BLOCK, inner))

        def advance(entering, block):
            block_inputs, block_state_inputs, block_in_map, block_state_map, block_out_map, block_step, block_decay, block_seg, before, block_gate = block
            y_intra, lead, state, carry = block_parts(block_inputs, block_state_inputs, block_in_map, block_state_map, block_out_map, block_step, block_decay, block_seg, before)
            values = block_output(y_intra, lead, entering, block_out_map, block_inputs, head_direct_gain)
            gated = gate_norm(values, block_gate, norm_weight)
            return (carry[:, None, None] * entering + state, (gated, entering))
        _, (gated, entering) = lax.scan(advance, jnp.zeros((HEADS, CHANNEL_WIDTH, STATE), jnp.float32), blocks)
        gated = gated.reshape(total_len, inner)
        ends = jnp.cumsum(length_row).astype(jnp.int32) - 1
        finals = []
        lasts = []
        for request in range(SEQS):
            spot = ends[request]
            index = spot // BLOCK
            start = (index * BLOCK).astype(jnp.int32)
            within = spot - start
            finals.append(state_at(lax.dynamic_slice_in_dim(state_inputs, start, BLOCK, 0), lax.dynamic_slice_in_dim(state_map, start, BLOCK, 0), lax.dynamic_slice_in_dim(step_size, start, BLOCK, 0), lax.dynamic_slice_in_dim(decays, start, BLOCK, 0), lax.dynamic_slice_in_dim(segment, start, BLOCK, 0), befores[index], within, entering[index]))
            lasts.append(gated[spot])
        return (gated, jnp.stack(finals), jnp.stack(lasts))
    y_gated, final_states, last_rows = lax.map(one_row, (conv_input, gate_projected, step_raw, lengths))
    flat_rows = last_rows.reshape(-1, inner)
    hidden = residual_last.reshape(-1, D).astype(jnp.float32) + jnp.dot(flat_rows, out_weight, preferred_element_type=jnp.float32)
    last_hidden = hidden.astype(jnp.bfloat16).reshape(residual_last.shape)
    scale = lax.rsqrt(lax.optimization_barrier(jnp.mean(hidden * hidden, axis=-1, keepdims=True)) + TINY_FLOOR)
    normed = (hidden * scale * final_gain).astype(jnp.bfloat16)
    pieces = vocab_weight.reshape(16, -1, D)

    def top_of(piece):
        logits = lax.dot_general(normed, piece, (((1,), (1,)), ((), ())), preferred_element_type=jnp.float32)
        return lax.optimization_barrier(jnp.max(logits, axis=1))
    tops = lax.map(top_of, pieces)
    max_logit = lax.optimization_barrier(jnp.max(tops, axis=0)).reshape(lengths.shape)
    return (y_gated, final_states, last_hidden, max_logit)
```

```python
import functools
import math

import jax
import jax.numpy as jnp
from jax import lax
from jax.experimental import pallas as pl
from jax.experimental.pallas import tpu as pltpu
from jax.sharding import PartitionSpec as P

D = 4096
HEADS = 64
WIDTH = 64
GROUPS = 4
STATE = 128
KERNEL = 4
SEQS = 4
INNER = HEADS * WIDTH
PER = HEADS // GROUPS
GW = INNER // GROUPS
Q = 128
EXTRA = 16
TINY_FLOOR = 1e-05
LOG2E = 1.0 / math.log(2.0)
BF = jnp.bfloat16
F32 = jnp.float32
HI = lax.Precision.HIGHEST
VM = 56 * 1024 * 1024


def params():
    return pltpu.CompilerParams(vmem_limit_bytes=VM)


def dot(a, b):
    return jnp.dot(a, b, preferred_element_type=F32)


def halves(x):
    hi = x.astype(BF)
    return hi, (x - hi.astype(F32)).astype(BF)


def spread(first_head, width):
    head = lax.broadcasted_iota(jnp.int32, (2 * HEADS, width), 0) % HEADS
    channel = lax.broadcasted_iota(jnp.int32, (2 * HEADS, width), 1)
    return (head == first_head + channel // WIDTH).astype(F32).astype(BF)


def silu(x):
    return x / (1.0 + jnp.exp(-x))


def segment(place, ends):
    return sum([(place >= ends[k]).astype(jnp.int32) for k in range(SEQS - 1)])


def prep_kernel(sc, dt_ref, log_ref, gain_ref, a_ref, b_ref, wst_ref, leadj_ref, lead0_ref, small_ref, cum, lj, l0, rows):
    T = dt_ref.shape[0]
    ends = [sc[k] for k in range(SEQS)]
    dt = dt_ref[...]
    dec = -jnp.exp(log_ref[...]) * dt
    later = lax.broadcasted_iota(jnp.int32, (T, T), 0)
    earlier = lax.broadcasted_iota(jnp.int32, (T, T), 1)
    total = jnp.dot((later >= earlier).astype(F32), dec, precision=HI, preferred_element_type=F32)
    cum[...] = total
    a2 = total * LOG2E
    for g in range(GROUPS):
        a_ref[g] = a2[:, g * PER : (g + 1) * PER]
    b_ref[...] = (a2 - jnp.log(dt) * LOG2E).T
    place = lax.broadcasted_iota(jnp.int32, (T, HEADS), 0)
    seg = segment(place, ends)
    lead0 = jnp.where(seg == segment(-1, ends), jnp.exp(total), 0.0)
    l0[...] = lead0
    stops = [cum[pl.ds(jnp.clip(ends[r] - 1, 0, T - 1), 1), :] for r in range(SEQS)]
    for j in range(T // Q):
        lo, hi = j * Q, (j + 1) * Q
        part = total[lo:hi]
        target = jnp.broadcast_to(total[hi - 1 : hi], (Q, HEADS))
        for r in range(SEQS - 1):
            target = jnp.where((seg[lo:hi] == r) & (ends[r] < hi), stops[r], target)
        weight = jnp.exp(target - part) * dt[lo:hi]
        wst_ref[lo:hi] = jnp.concatenate(halves(weight), axis=1)
        base = total[lo - 1 : lo] if j else 0.0
        lead = jnp.where(seg[lo:hi] == segment(lo - 1, ends), jnp.exp(part - base), 0.0)
        lj[lo:hi] = lead
        rows[j : j + 1] = lead[Q - 1 :]
    leadj_ref[...] = jnp.concatenate(halves(lj[...]), axis=1)
    lead0_ref[...] = jnp.concatenate(halves(lead0), axis=1)
    n = T // Q
    for r in range(SEQS):
        stop = ends[r] - 1
        owned = ((stop >= 0) & (stop < T)).astype(F32)
        at = pl.ds(jnp.clip(stop, 0, T - 1), 1)
        rows[n + r : n + r + 1] = lj[at, :] * owned
        rows[n + SEQS + r : n + SEQS + r + 1] = l0[at, :] * owned
    rows[n + 2 * SEQS : n + 2 * SEQS + 1] = lead0[T - 1 :]
    rows[n + 2 * SEQS + 1 : n + 2 * SEQS + 2] = gain_ref[...]
    small_ref[...] = jnp.concatenate(halves(rows[...]), axis=1)


def prep(scalars, dt, decay_log, gain):
    T = dt.shape[0]
    nrows = -(-(T // Q + 2 * SEQS + 2) // 16) * 16
    sds = jax.ShapeDtypeStruct
    return pl.pallas_call(
        prep_kernel,
        in_specs=[pl.BlockSpec(memory_space=pltpu.SMEM)] + [pl.BlockSpec(memory_space=pltpu.VMEM)] * 3,
        out_specs=[pl.BlockSpec(memory_space=pltpu.VMEM)] * 6,
        out_shape=[
            sds((GROUPS, T, PER), F32),
            sds((HEADS, T), F32),
            sds((T, 2 * HEADS), BF),
            sds((T, 2 * HEADS), BF),
            sds((T, 2 * HEADS), BF),
            sds((nrows, 2 * HEADS), BF),
        ],
        scratch_shapes=[
            pltpu.VMEM((T, HEADS), F32),
            pltpu.VMEM((T, HEADS), F32),
            pltpu.VMEM((T, HEADS), F32),
            pltpu.VMEM((nrows, HEADS), F32),
        ],
        compiler_params=params(),
        name="prep",
    )(scalars, dt, decay_log, gain)


def front_kernel(seqs, shard_w, sc, x_ref, b_ref, c_ref, hx, hb, hc, wx, wb, wc, bx, bb, bc, wst, small, gate,
                 xm, bm, cm, pay, eloc, slots, xs, act, ent, exs):
    T = x_ref.shape[0]
    n = T // Q
    g = pl.program_id(0)
    ends = [sc[k] for k in range(SEQS)]
    span = sc[SEQS]
    shards = GW // shard_w
    cuts = [slice(k * shard_w, (k + 1) * shard_w) for k in range(shards)]
    R = spread(g * PER, GW)
    wide = dot(small[...], R)
    packed = small[...].astype(F32)
    gain = wide[n + 2 * SEQS + 1 : n + 2 * SEQS + 2]
    pieces = [
        (x_ref, hx, wx, bx, xm, 0, GW),
        (b_ref, hb, wb, bb, bm, GW, STATE),
        (c_ref, hc, wc, bc, cm, GW + STATE, STATE),
    ]
    for src, halo, _, _, _, at, w in pieces:
        xs[0:8, at : at + w] = halo[...]
        xs[8:, at : at + w] = src[...].astype(F32)
    ent[...] = jnp.zeros_like(ent)
    slots[...] = jnp.zeros_like(slots)
    exs[...] = jnp.zeros_like(exs)
    for k in range(shards):
        exs[k, SEQS : 2 * SEQS, :] = gate[0:SEQS, cuts[k]]
        exs[k, 3 * SEQS : 3 * SEQS + 1, 0:128] = packed[n + 2 * SEQS : n + 2 * SEQS + 1]

    for j in range(n):
        lo = j * Q
        place = lo + lax.broadcasted_iota(jnp.int32, (Q, 128), 0)
        here = segment(place, ends)
        same = [(segment(place - 3 + k, ends) == here).astype(F32) for k in range(KERNEL - 1)]
        for src, _, w_ref, bias, out, at, w in pieces:
            for c in range(0, w, 128):
                col = slice(at + c, at + c + 128)
                acc = jnp.broadcast_to(bias[:, c : c + 128], (Q, 128))
                for k in range(KERNEL):
                    tap = w_ref[k : k + 1, c : c + 128] * xs[lo + 5 + k : lo + 5 + k + Q, col]
                    acc = acc + (tap * same[k] if k < KERNEL - 1 else tap)
                y = silu(acc)
                act[lo : lo + Q, col] = y
                out[lo : lo + Q, c : c + 128] = y.astype(BF)
        scaled = act[lo : lo + Q, :GW] * dot(wst[lo : lo + Q], R)
        xhi, xlo = halves(scaled)
        right = jnp.concatenate([xhi, xlo, xhi], axis=0)
        bt = act[lo : lo + Q, GW : GW + STATE].T
        lane_seg = segment(lo + lax.broadcasted_iota(jnp.int32, (STATE, Q), 1), ends)

        def gathered(which, bt=bt, lane_seg=lane_seg, right=right):
            bhi, blo = halves(jnp.where(lane_seg == which, bt, 0.0))
            return dot(jnp.concatenate([bhi, bhi, blo], axis=1), right)

        if j:
            eloc[j - 1] = ent[...].astype(BF)
        for r in range(SEQS):
            stop = ends[r] - 1

            @pl.when((stop >= lo) & (stop < lo + Q))
            def _(r=r, stop=stop, gathered=gathered):
                tail = wide[n + r : n + r + 1] * ent[...] + gathered(r)
                if r < SEQS - 1:
                    keep = stop < T - 1
                    if r != 1:
                        keep = keep & ((span < seqs // 2) if r == 0 else (span >= seqs // 2))

                    @pl.when(keep)
                    def _():
                        for k in range(shards):
                            slots[k, r % 2] = tail[:, cuts[k]].astype(BF)

                row = act[pl.ds(stop, 1), :].astype(BF)
                out_map = jnp.broadcast_to(row[:, GW + STATE :], (16, STATE))
                thi, tlo = halves(tail)
                value = (dot(out_map, thi) + dot(out_map, tlo))[0:1]
                value = value + gain * row[:, :GW].astype(F32)
                for k in range(shards):
                    exs[k, r : r + 1, :] = value[:, cuts[k]]
                    exs[k, 2 * SEQS + r : 2 * SEQS + r + 1, 0:128] = row[:, GW + STATE :].astype(F32)
                    exs[k, 2 * SEQS + r : 2 * SEQS + r + 1, 128:256] = packed[n + SEQS + r : n + SEQS + r + 1]

        ent[...] = wide[j : j + 1] * ent[...] + gathered(segment(lo + Q - 1, ends))
    for k in range(shards):
        pay[k, 0:STATE, :] = ent[:, cuts[k]].astype(BF)
        pay[k, STATE:, :] = exs[k].astype(BF)


def front(scalars, rows, halo, conv_weight, bias, wst, small, gate_rows, seqs):
    T = rows.shape[0]
    shard_w = INNER // seqs
    shards = GW // shard_w
    n = T // Q
    first_b, first_c = INNER // STATE, INNER // STATE + GROUPS
    sds = jax.ShapeDtypeStruct

    def three(height):
        return [
            pl.BlockSpec((height, GW), lambda g: (0, g)),
            pl.BlockSpec((height, STATE), lambda g: (0, first_b + g)),
            pl.BlockSpec((height, STATE), lambda g: (0, first_c + g)),
        ]

    whole = lambda a: pl.BlockSpec(a.shape, lambda g: (0, 0))
    return pl.pallas_call(
        functools.partial(front_kernel, seqs, shard_w),
        grid=(GROUPS,),
        in_specs=[pl.BlockSpec(memory_space=pltpu.SMEM)]
        + three(T)
        + three(8)
        + three(KERNEL)
        + three(1)
        + [whole(wst), whole(small), pl.BlockSpec((gate_rows.shape[0], GW), lambda g: (0, g))],
        out_specs=[
            pl.BlockSpec((T, GW), lambda g: (0, g)),
            pl.BlockSpec((T, STATE), lambda g: (0, g)),
            pl.BlockSpec((T, STATE), lambda g: (0, g)),
            pl.BlockSpec((shards, STATE + EXTRA, shard_w), lambda g: (g, 0, 0)),
            pl.BlockSpec((n - 1, STATE, GW), lambda g: (0, 0, g)),
            pl.BlockSpec((shards, 2, STATE, shard_w), lambda g: (g, 0, 0, 0)),
        ],
        out_shape=[
            sds((T, INNER), BF),
            sds((T, GROUPS * STATE), BF),
            sds((T, GROUPS * STATE), BF),
            sds((seqs, STATE + EXTRA, shard_w), BF),
            sds((n - 1, STATE, INNER), BF),
            sds((seqs, 2, STATE, shard_w), BF),
        ],
        scratch_shapes=[
            pltpu.VMEM((T + 8, GW + 2 * STATE), F32),
            pltpu.VMEM((T, GW + 2 * STATE), F32),
            pltpu.VMEM((STATE, GW), F32),
            pltpu.VMEM((shards, EXTRA, shard_w), F32),
        ],
        compiler_params=params(),
        name="front",
    )(scalars, rows, rows, rows, halo, halo, halo, conv_weight, conv_weight, conv_weight, bias, bias, bias, wst, small, gate_rows)


def local_kernel(gain_row, sc, x_ref, b_ref, c_ref, a_ref, bt_ref, lead, eloc, small, out):
    g, j = pl.program_id(0), pl.program_id(1)
    ends = [sc[k] for k in range(SEQS)]
    R = spread(g * PER, GW)
    wide = dot(small[...], R)
    gain = wide[gain_row : gain_row + 1]
    t = j * Q + lax.broadcasted_iota(jnp.int32, (Q, Q), 0)
    s = j * Q + lax.broadcasted_iota(jnp.int32, (Q, Q), 1)
    out_map = c_ref[...]
    scores = lax.dot_general(out_map, b_ref[...], (((1,), (1,)), ((), ())), preferred_element_type=F32)
    scores = jnp.where((s <= t) & (segment(t, ends) == segment(s, ends)), scores, 0.0)
    a, b = a_ref[0], bt_ref[...]
    low = (lax.broadcasted_iota(jnp.int32, (Q, 2 * WIDTH), 1) < WIDTH).astype(F32).astype(BF)
    high = 1 - low

    for p in range(PER // 2):
        col = slice(2 * p * WIDTH, 2 * (p + 1) * WIDTH)
        m = [
            (jnp.exp2(jnp.minimum(a[:, h : h + 1] - b[h : h + 1, :], 60.0)) * scores).astype(BF)
            for h in (2 * p, 2 * p + 1)
        ]
        x = x_ref[:, col]
        y = dot(jnp.concatenate(m, axis=1), jnp.concatenate([x * low, x * high], axis=0))
        out[:, col] = y + gain[:, col] * x.astype(F32)

    @pl.when(j > 0)
    def _():
        out[...] += dot(lead[...], R) * dot(out_map, eloc[0])


def local(scalars, xm, bm, cm, a2, b2, lead, eloc, small):
    T = xm.shape[0]
    return pl.pallas_call(
        functools.partial(local_kernel, T // Q + 2 * SEQS + 1),
        grid=(GROUPS, T // Q),
        in_specs=[
            pl.BlockSpec(memory_space=pltpu.SMEM),
            pl.BlockSpec((Q, GW), lambda g, j: (j, g)),
            pl.BlockSpec((Q, STATE), lambda g, j: (j, g)),
            pl.BlockSpec((Q, STATE), lambda g, j: (j, g)),
            pl.BlockSpec((1, Q, PER), lambda g, j: (g, j, 0)),
            pl.BlockSpec((PER, Q), lambda g, j: (g, j)),
            pl.BlockSpec((Q, 2 * HEADS), lambda g, j: (j, 0)),
            pl.BlockSpec((1, STATE, GW), lambda g, j: (jnp.maximum(j - 1, 0), 0, g)),
            pl.BlockSpec(small.shape, lambda g, j: (0, 0)),
        ],
        out_specs=pl.BlockSpec((Q, GW), lambda g, j: (j, g)),
        out_shape=jax.ShapeDtypeStruct((T, INNER), F32),
        compiler_params=params(),
        cost_estimate=pl.CostEstimate(flops=8 * 10**9, bytes_accessed=2 * 10**7, transcendentals=5 * 10**6),
        name="local",
    )(scalars, xm, bm, cm, a2, b2, lead, eloc, small)


def scan_kernel(sc, got, enter, base, value, ent):
    seqs, _, shard_w = got.shape
    R = spread(sc[2 * SEQS] * (shard_w // WIDTH), shard_w)
    ent[...] = jnp.zeros_like(ent)
    value[...] = jnp.zeros_like(value)
    for i in range(seqs):
        now = ent[...]
        enter[i] = now.astype(BF)
        state = got[i, 0:STATE].astype(F32)
        extra = got[i, STATE:]
        carry = dot(extra[:, 0:128], R)[3 * SEQS : 3 * SEQS + 1]
        for r in range(SEQS):

            @pl.when(sc[r] == i)
            def _(r=r, now=now, state=state, extra=extra):
                at = slice(2 * SEQS + r, 2 * SEQS + r + 1)
                lead = dot(extra[:, 128:256], R)[at]
                base[r] = lead * now + jnp.where(sc[SEQS + r] == 1, state, 0.0)
                hi, lo = halves(now)
                inter = (dot(extra[:, 0:128], hi) + dot(extra[:, 0:128], lo))[at]
                rows = extra.astype(F32)
                value[r : r + 1, :] = (rows[r : r + 1] + lead * inter) * silu(rows[SEQS + r : SEQS + r + 1])

        ent[...] = carry * now + state


def scan(scalars, got):
    seqs, _, shard_w = got.shape
    sds = jax.ShapeDtypeStruct
    return pl.pallas_call(
        scan_kernel,
        in_specs=[pl.BlockSpec(memory_space=pltpu.SMEM), pl.BlockSpec(memory_space=pltpu.VMEM)],
        out_specs=[pl.BlockSpec(memory_space=pltpu.VMEM)] * 3,
        out_shape=[
            sds((seqs, STATE, shard_w), BF),
            sds((SEQS, STATE, shard_w), F32),
            sds((8, shard_w), F32),
        ],
        scratch_shapes=[pltpu.VMEM((STATE, shard_w), F32)],
        compiler_params=params(),
        name="scan",
    )(scalars, got)


def finals_kernel(sc, base, tail, out):
    r = pl.program_id(0)
    use = (r < SEQS - 1) & (sc[SEQS + r] == 0)
    out[0] = (base[0] + jnp.where(use, tail[0, 0].astype(F32), 0.0)).T


def finals(scalars, base, tails):
    _, _, shard_w = base.shape
    return pl.pallas_call(
        finals_kernel,
        grid_spec=pltpu.PrefetchScalarGridSpec(
            num_scalar_prefetch=1,
            grid=(SEQS,),
            in_specs=[
                pl.BlockSpec((1, STATE, shard_w), lambda r, sc: (r, 0, 0)),
                pl.BlockSpec((1, 1, STATE, shard_w), lambda r, sc: (sc[r], r % 2, 0, 0)),
            ],
            out_specs=pl.BlockSpec((1, shard_w, STATE), lambda r, sc: (r, 0, 0)),
        ),
        out_shape=jax.ShapeDtypeStruct((SEQS, shard_w, STATE), F32),
        compiler_params=params(),
        name="finals",
    )(scalars, base, tails)


def finish_kernel(y_ref, gate, c_ref, e_ref, lead, norm, out):
    R = spread(pl.program_id(0) * PER, GW)
    entering = jnp.concatenate([e_ref[k] for k in range(e_ref.shape[0])], axis=1)
    y = y_ref[...] + dot(lead[...], R) * dot(c_ref[...], entering)
    v = y * silu(gate[...].astype(F32))
    scale = lax.rsqrt(jnp.sum(v * v, axis=1, keepdims=True) * (1.0 / GW) + TINY_FLOOR)
    out[...] = (v * scale * norm[...]).astype(BF)


def finish(y_local, gate, cm, enter, lead, norm):
    T = y_local.shape[0]
    seqs, _, shard_w = enter.shape
    tile = 256
    return pl.pallas_call(
        finish_kernel,
        grid=(GROUPS, T // tile),
        in_specs=[
            pl.BlockSpec((tile, GW), lambda g, i: (i, g)),
            pl.BlockSpec((tile, GW), lambda g, i: (i, g)),
            pl.BlockSpec((tile, STATE), lambda g, i: (i, g)),
            pl.BlockSpec((GW // shard_w, STATE, shard_w), lambda g, i: (g, 0, 0)),
            pl.BlockSpec((tile, 2 * HEADS), lambda g, i: (i, 0)),
            pl.BlockSpec((1, GW), lambda g, i: (0, g)),
        ],
        out_specs=pl.BlockSpec((tile, GW), lambda g, i: (i, g)),
        out_shape=jax.ShapeDtypeStruct((T, INNER), BF),
        compiler_params=params(),
        cost_estimate=pl.CostEstimate(flops=2 * 10**9, bytes_accessed=2 * 10**7, transcendentals=4 * 10**6),
        name="finish",
    )(y_local, gate, cm, enter, lead, norm)


def exchange(x, axes):
    return lax.all_to_all(x, axes, 0, 0, tiled=True)


def body(
    conv_input,
    gate_projected,
    step_raw,
    step_bias,
    decay_log,
    head_direct_gain,
    conv_weight,
    convolution_bias,
    norm_weight,
    lengths,
    out_weight,
    residual_last,
    final_gain,
    vocab_weight,
):
    every = ("req", "seq")
    T = conv_input.shape[1]
    seqs, reqs = lax.axis_size("seq"), lax.axis_size("req")
    seq_place, req_place = lax.axis_index("seq"), lax.axis_index("req")
    devices = seqs * reqs
    flat = req_place * seqs + seq_place
    shard_w = INNER // seqs
    share = out_weight.shape[0]
    rows_total = reqs * SEQS
    rows = conv_input[0]

    edge = lax.ppermute(rows[T - (KERNEL - 1) :], "seq", [(i, i + 1) for i in range(seqs - 1)])
    halo = jnp.pad(edge.astype(F32), ((8 - (KERNEL - 1), 0), (0, 0)))
    ends = jnp.cumsum(lengths[0]).astype(jnp.int32)
    local_ends = ends - seq_place * T
    scalars = jnp.concatenate([local_ends, seq_place[None].astype(jnp.int32)])
    last = ends - 1
    owner = last // T
    at_end = (ends % T == 0).astype(jnp.int32)
    owners = jnp.concatenate([owner, at_end, seq_place[None].astype(jnp.int32)])

    dt = jax.nn.softplus(step_raw[0] + step_bias)
    stop = local_ends - 1
    owned = (stop >= 0) & (stop < T)
    gate_rows = gate_projected[0][jnp.clip(stop, 0, T - 1)].astype(F32)
    gate_rows = jnp.pad(jnp.where(owned[:, None], gate_rows, 0.0), ((0, 8 - SEQS), (0, 0)))

    a2, b2, wst, leadj, lead0, small = prep(scalars, dt, decay_log[None], head_direct_gain[None])
    xm, bm, cm, pay, eloc, slots = front(
        scalars, rows, halo, conv_weight, convolution_bias[None], wst, small, gate_rows, seqs
    )
    got = exchange(pay, "seq")
    y_local = local(scalars, xm, bm, cm, a2, b2, leadj, eloc, small)
    enter, base, value = scan(owners, got)
    entering = exchange(enter, "seq")

    parts = shard_w // share
    mine = value[:SEQS].reshape(SEQS, parts, share).transpose(1, 0, 2)
    mail = lax.dynamic_update_slice(jnp.zeros((devices, SEQS, share), F32), mine, (seq_place * parts, 0, 0))
    mail = exchange(mail, every).reshape(reqs, seqs, SEQS, share)
    v = lax.dynamic_index_in_dim(mail, flat * share // shard_w, 1, keepdims=False).reshape(rows_total, share)
    squares = jnp.sum(v * v, axis=1)
    u = (v * lax.dynamic_slice_in_dim(norm_weight, flat * share, share)).astype(BF)
    partial = jnp.dot(u, out_weight, preferred_element_type=F32)
    chunk = D // devices
    mail = partial.reshape(rows_total, devices, chunk).transpose(1, 0, 2)
    line = jnp.pad(squares, (0, chunk - rows_total))
    mail = jnp.concatenate([mail, jnp.broadcast_to(line, (devices, 8, chunk))], axis=1)
    mail = exchange(mail, every)
    sums = mail.reshape(GROUPS, devices // GROUPS, rows_total + 8, chunk).sum(axis=1)
    scale = lax.rsqrt(sums[:, rows_total, :rows_total] * (1.0 / GW) + TINY_FLOOR)
    own = jnp.sum(scale[:, :, None] * sums[:, :rows_total], axis=0)
    residual = residual_last.reshape(rows_total, D)
    own = own + lax.dynamic_slice_in_dim(residual, flat * chunk, chunk, 1).astype(F32)
    mail = exchange(jnp.broadcast_to(own, (devices, rows_total, chunk)), every)
    hidden = mail.transpose(1, 0, 2).reshape(rows_total, D)
    rms = lax.rsqrt(jnp.mean(hidden * hidden, axis=-1, keepdims=True) + TINY_FLOOR)
    normed = (hidden * rms * final_gain).astype(BF)
    last_hidden = lax.dynamic_slice_in_dim(hidden.reshape(reqs, SEQS, D), req_place, 1, 0).astype(BF)

    y_gated = finish(y_local, gate_projected[0], cm, entering, lead0, norm_weight[None])

    logits = lax.dot_general(normed, vocab_weight, (((1,), (1,)), ((), ())), preferred_element_type=F32)
    top = jnp.max(logits, axis=1).reshape(reqs, 1, SEQS)
    top = jnp.broadcast_to(top, (reqs, seqs, SEQS)).reshape(devices, SEQS)
    max_logit = jnp.max(exchange(top, every), axis=0, keepdims=True)

    tails = exchange(slots, "seq")
    final_states = finals(owners, base, tails).reshape(1, SEQS, HEADS // seqs, WIDTH, STATE)
    return (y_gated[None], final_states, last_hidden, max_logit)


def solution(mesh):
    return jax.shard_map(
        body,
        mesh=mesh,
        in_specs=(
            P("req", "seq", None),
            P("req", "seq", None),
            P("req", "seq", None),
            P(),
            P(),
            P(),
            P(),
            P(),
            P(),
            P("req", None),
            P(("req", "seq"), None),
            P(),
            P(),
            P(("req", "seq"), None),
        ),
        out_specs=(
            P("req", "seq", None),
            P("req", None, "seq", None, None),
            P("req", None, None),
            P("req", None),
        ),
        check_vma=False,
    )
```

```python
import functools
import math

import jax
import jax.numpy as jnp
from jax import lax
from jax.experimental import pallas as pl
from jax.experimental.pallas import tpu as pltpu
from jax.sharding import PartitionSpec as P

D = 4096
HEADS = 64
WIDTH = 64
GROUPS = 4
STATE = 128
KERNEL = 4
SEQS = 4
INNER = HEADS * WIDTH
PER = HEADS // GROUPS
GW = INNER // GROUPS
Q = 128
EXTRA = 16
TINY_FLOOR = 1e-05
LOG2E = 1.0 / math.log(2.0)
BF = jnp.bfloat16
F32 = jnp.float32
HI = lax.Precision.HIGHEST
VM = 56 * 1024 * 1024


def params():
    return pltpu.CompilerParams(vmem_limit_bytes=VM)


def dot(a, b):
    return jnp.dot(a, b, preferred_element_type=F32)


def halves(x):
    hi = x.astype(BF)
    return hi, (x - hi.astype(F32)).astype(BF)


def spread(first_head, width):
    head = lax.broadcasted_iota(jnp.int32, (2 * HEADS, width), 0) % HEADS
    channel = lax.broadcasted_iota(jnp.int32, (2 * HEADS, width), 1)
    return (head == first_head + channel // WIDTH).astype(F32).astype(BF)


def silu(x):
    half = 0.5 * x
    return half + half * jnp.tanh(half)


def stops(lengths, me, T):
    total, ends = -me[0] * T, []
    for k in range(SEQS):
        total = total + lengths[k]
        ends.append(total)
    return ends


def segment(place, ends):
    return sum([(place >= ends[k]).astype(jnp.int32) for k in range(SEQS - 1)])


def prep_kernel(lengths, me, raw_ref, bias_ref, log_ref, gain_ref, a_ref, b_ref, wst_ref, leadj_ref, lead0_ref, pick_ref, small_ref, cum, lj, l0, rows):
    T = raw_ref.shape[1]
    ends = stops(lengths, me, T)
    z = raw_ref[...] + jnp.broadcast_to(bias_ref[...], (8, HEADS)).T[:, 0:1]
    u = jnp.exp(-jnp.abs(z))
    series = u * (1.0 - u * (0.5 - u * (1.0 / 3.0 - u * (0.25 - u * 0.2))))
    dt_t = jnp.maximum(z, 0.0) + jnp.where(u < 0.03, series, jnp.log(1.0 + u))
    dec = -jnp.exp(jnp.broadcast_to(log_ref[...], (8, HEADS)).T[:, 0:1]) * dt_t
    earlier = lax.broadcasted_iota(jnp.int32, (T, T), 0)
    later = lax.broadcasted_iota(jnp.int32, (T, T), 1)
    total_t = jnp.dot(dec, (later >= earlier).astype(F32), precision=HI, preferred_element_type=F32)
    b_ref[...] = (total_t - jnp.log(dt_t)) * LOG2E
    total, dt = total_t.T, dt_t.T
    cum[...] = total
    a2 = total * LOG2E
    for g in range(GROUPS):
        a_ref[g] = a2[:, g * PER : (g + 1) * PER]
    place = lax.broadcasted_iota(jnp.int32, (T, HEADS), 0)
    seg = segment(place, ends)
    lead0 = jnp.where(seg == segment(-1, ends), jnp.exp(total), 0.0)
    l0[...] = lead0
    target = lax.broadcasted_iota(jnp.int32, (Q, Q + 16), 0)
    source = lax.broadcasted_iota(jnp.int32, (Q, Q + 16), 1) - 16
    for j in range(T // Q):
        same = segment(j * Q + target, ends) == segment(j * Q + source, ends)
        for k in range(KERNEL - 1):
            chosen = same & (source == target + (k - (KERNEL - 1)))
            pick_ref[j, k * Q : (k + 1) * Q] = chosen.astype(F32).astype(BF)
    at_stop = [cum[pl.ds(jnp.clip(ends[r] - 1, 0, T - 1), 1), :] for r in range(SEQS)]
    for j in range(T // Q):
        lo, hi = j * Q, (j + 1) * Q
        part = total[lo:hi]
        aim = jnp.broadcast_to(total[hi - 1 : hi], (Q, HEADS))
        for r in range(SEQS - 1):
            aim = jnp.where((seg[lo:hi] == r) & (ends[r] < hi), at_stop[r], aim)
        weight = jnp.exp(aim - part) * dt[lo:hi]
        wst_ref[lo:hi] = jnp.concatenate(halves(weight), axis=1)
        base = total[lo - 1 : lo] if j else 0.0
        lead = jnp.where(seg[lo:hi] == segment(lo - 1, ends), jnp.exp(part - base), 0.0)
        lj[lo:hi] = lead
        rows[j : j + 1] = lead[Q - 1 :]
    leadj_ref[...] = jnp.concatenate(halves(lj[...]), axis=1)
    lead0_ref[...] = jnp.concatenate(halves(lead0), axis=1)
    n = T // Q
    for r in range(SEQS):
        stop = ends[r] - 1
        owned = ((stop >= 0) & (stop < T)).astype(F32)
        at = pl.ds(jnp.clip(stop, 0, T - 1), 1)
        rows[n + r : n + r + 1] = lj[at, :] * owned
        rows[n + SEQS + r : n + SEQS + r + 1] = l0[at, :] * owned
    rows[n + 2 * SEQS : n + 2 * SEQS + 1] = lead0[T - 1 :]
    rows[n + 2 * SEQS + 1 : n + 2 * SEQS + 2] = gain_ref[...]
    small_ref[...] = jnp.concatenate(halves(rows[...]), axis=1)


SMEM = pl.BlockSpec(memory_space=pltpu.SMEM)
VMEM = pl.BlockSpec(memory_space=pltpu.VMEM)


def prep(lengths, me, raw, bias, decay_log, gain):
    T = raw.shape[1]
    nrows = -(-(T // Q + 2 * SEQS + 2) // 16) * 16
    sds = jax.ShapeDtypeStruct
    return pl.pallas_call(
        prep_kernel,
        in_specs=[SMEM, SMEM] + [VMEM] * 4,
        out_specs=[VMEM] * 7,
        out_shape=[
            sds((GROUPS, T, PER), F32),
            sds((HEADS, T), F32),
            sds((T, 2 * HEADS), BF),
            sds((T, 2 * HEADS), BF),
            sds((T, 2 * HEADS), BF),
            sds((T // Q, (KERNEL - 1) * Q, Q + 16), BF),
            sds((nrows, 2 * HEADS), BF),
        ],
        scratch_shapes=[
            pltpu.VMEM((T, HEADS), F32),
            pltpu.VMEM((T, HEADS), F32),
            pltpu.VMEM((T, HEADS), F32),
            pltpu.VMEM((nrows, HEADS), F32),
        ],
        compiler_params=params(),
        name="prep",
    )(lengths, me, raw, bias, decay_log, gain)


def front_kernel(seqs, shard_w, lengths, me, x_ref, b_ref, c_ref, hx, hb, hc, wx, wb, wc, bx, bb, bc, wst, pick, small, gate,
                 xm, bm, cm, pay, eloc, keep0, keep1, give0, give1, act, ent, exs, near, sems):
    slots = ((keep0, keep1), (give0, give1))
    T = x_ref.shape[0]
    n = T // Q
    g = pl.program_id(0)
    ends = stops(lengths, me, T)
    span = me[0]
    shards = GW // shard_w
    cuts = [slice(k * shard_w, (k + 1) * shard_w) for k in range(shards)]
    R = spread(g * PER, GW)
    wide = dot(small[...], R)
    packed = small[...].astype(F32)
    gain = wide[n + 2 * SEQS + 1 : n + 2 * SEQS + 2]
    pieces = [
        (x_ref, hx, wx, bx, xm, 0, GW),
        (b_ref, hb, wb, bb, bm, GW, STATE),
        (c_ref, hc, wc, bc, cm, GW + STATE, STATE),
    ]
    spots = [jnp.clip(ends[r] - 1, 0, T - 1) for r in range(SEQS)]

    def fetch(r):
        top = pl.multiple_of(spots[r] // 16 * 16, 16)
        cols = pl.ds(pl.multiple_of(g * GW, GW), GW)
        return pltpu.make_async_copy(gate.at[pl.ds(top, 16), cols], near.at[r], sems.at[r])

    for r in range(SEQS):
        fetch(r).start()
    ent[...] = jnp.zeros_like(ent)
    for slot in slots[0] + slots[1]:
        slot[...] = jnp.zeros_like(slot)
    exs[...] = jnp.zeros_like(exs)
    for k in range(shards):
        exs[k, 3 * SEQS : 3 * SEQS + 1, 0:128] = packed[n + 2 * SEQS : n + 2 * SEQS + 1]

    for j in range(n):
        lo = j * Q
        for src, halo, w_ref, bias, out, at, w in pieces:
            own = src[lo : lo + Q]
            window = jnp.concatenate([src[lo - 16 : lo] if j else halo[...], own], axis=0)
            for c in range(0, w, 256):
                c2 = min(c + 256, w)
                near3 = dot(pick[j], window[:, c:c2])
                acc = bias[:, c:c2] + w_ref[KERNEL - 1 : KERNEL, c:c2] * own[:, c:c2].astype(F32)
                for k in range(KERNEL - 1):
                    acc = acc + w_ref[k : k + 1, c:c2] * near3[k * Q : (k + 1) * Q]
                y = silu(acc)
                act[lo : lo + Q, at + c : at + c2] = y
                out[lo : lo + Q, c:c2] = y.astype(BF)
        scaled = act[lo : lo + Q, :GW] * dot(wst[lo : lo + Q], R)
        xhi, xlo = halves(scaled)
        right = jnp.concatenate([xhi, xlo, xhi], axis=0)
        bt = act[lo : lo + Q, GW : GW + STATE].T
        lane_seg = segment(lo + lax.broadcasted_iota(jnp.int32, (STATE, Q), 1), ends)

        def gathered(which, bt=bt, lane_seg=lane_seg, right=right):
            bhi, blo = halves(jnp.where(lane_seg == which, bt, 0.0))
            return dot(jnp.concatenate([bhi, bhi, blo], axis=1), right)

        if j:
            eloc[j - 1] = ent[...].astype(BF)
        for r in range(SEQS):
            stop = ends[r] - 1

            @pl.when((stop >= lo) & (stop < lo + Q))
            def _(r=r, stop=stop, gathered=gathered):
                tail = wide[n + r : n + r + 1] * ent[...] + gathered(r)
                if r < SEQS - 1:
                    fits = stop < T - 1
                    if r != 1:
                        fits = fits & ((span < seqs // 2) if r == 0 else (span >= seqs // 2))
                    for p in range(2):

                        @pl.when(fits & (span % 2 == p))
                        def _(p=p):
                            for k in range(shards):
                                to = slots[0 if k % 2 == p else 1][r % 2]
                                to[k // 2] = tail[:, cuts[k]].astype(BF)

                row = act[pl.ds(stop, 1), :].astype(BF)
                out_map = jnp.broadcast_to(row[:, GW + STATE :], (16, STATE))
                thi, tlo = halves(tail)
                value = (dot(out_map, thi) + dot(out_map, tlo))[0:1]
                value = value + gain * row[:, :GW].astype(F32)
                for k in range(shards):
                    exs[k, r : r + 1, :] = value[:, cuts[k]]
                    exs[k, 2 * SEQS + r : 2 * SEQS + r + 1, 0:128] = row[:, GW + STATE :].astype(F32)
                    exs[k, 2 * SEQS + r : 2 * SEQS + r + 1, 128:256] = packed[n + SEQS + r : n + SEQS + r + 1]

        ent[...] = wide[j : j + 1] * ent[...] + gathered(segment(lo + Q - 1, ends))
    for r in range(SEQS):
        fetch(r).wait()
        mine = lax.broadcasted_iota(jnp.int32, (16, GW), 0) == spots[r] % 16
        owned = (spots[r] == ends[r] - 1).astype(F32)
        line = jnp.sum(jnp.where(mine, near[r].astype(F32), 0.0), axis=0, keepdims=True) * owned
        for k in range(shards):
            exs[k, SEQS + r : SEQS + r + 1, :] = line[:, cuts[k]]
    for k in range(shards):
        pay[k, 0:STATE, :] = ent[:, cuts[k]].astype(BF)
        pay[k, STATE:, :] = exs[k].astype(BF)


def front(lengths, me, rows, halo, conv_weight, bias, wst, pick, small, gate, seqs):
    T = rows.shape[0]
    shard_w = INNER // seqs
    shards = GW // shard_w
    n = T // Q
    first_b, first_c = INNER // STATE, INNER // STATE + GROUPS
    sds = jax.ShapeDtypeStruct

    def three(height):
        return [
            pl.BlockSpec((height, GW), lambda g: (0, g)),
            pl.BlockSpec((height, STATE), lambda g: (0, first_b + g)),
            pl.BlockSpec((height, STATE), lambda g: (0, first_c + g)),
        ]

    whole = lambda a: pl.BlockSpec(a.shape, lambda g: (0, 0))
    return pl.pallas_call(
        functools.partial(front_kernel, seqs, shard_w),
        grid=(GROUPS,),
        in_specs=[SMEM, SMEM]
        + three(T)
        + three(16)
        + three(KERNEL)
        + three(1)
        + [whole(wst), pl.BlockSpec(pick.shape, lambda g: (0, 0, 0)), whole(small), pl.BlockSpec(memory_space=pl.ANY)],
        out_specs=[
            pl.BlockSpec((T, GW), lambda g: (0, g)),
            pl.BlockSpec((T, STATE), lambda g: (0, g)),
            pl.BlockSpec((T, STATE), lambda g: (0, g)),
            pl.BlockSpec((shards, STATE + EXTRA, shard_w), lambda g: (g, 0, 0)),
            pl.BlockSpec((n - 1, STATE, GW), lambda g: (0, 0, g)),
        ]
        + [pl.BlockSpec((shards // 2, STATE, shard_w), lambda g: (g, 0, 0))] * 4,
        out_shape=[
            sds((T, INNER), BF),
            sds((T, GROUPS * STATE), BF),
            sds((T, GROUPS * STATE), BF),
            sds((seqs, STATE + EXTRA, shard_w), BF),
            sds((n - 1, STATE, INNER), BF),
        ]
        + [sds((seqs // 2, STATE, shard_w), BF)] * 4,
        scratch_shapes=[
            pltpu.VMEM((T, GW + 2 * STATE), F32),
            pltpu.VMEM((STATE, GW), F32),
            pltpu.VMEM((shards, EXTRA, shard_w), F32),
            pltpu.VMEM((SEQS, 16, GW), BF),
            pltpu.SemaphoreType.DMA((SEQS,)),
        ],
        compiler_params=params(),
        name="front",
    )(lengths, me, rows, rows, rows, halo, halo, halo, conv_weight, conv_weight, conv_weight, bias, bias, bias, wst, pick, small, gate)


def local_kernel(gain_row, lengths, me, x_ref, b_ref, c_ref, a_ref, bt_ref, lead, eloc, small, out):
    T = x_ref.shape[0]
    ends = stops(lengths, me, T)
    R = spread(pl.program_id(0) * PER, GW)
    wide = dot(small[...], R)
    gain = wide[gain_row : gain_row + 1]
    low = (lax.broadcasted_iota(jnp.int32, (Q, 2 * WIDTH), 1) < WIDTH).astype(F32).astype(BF)
    high = 1 - low
    for j in range(T // Q):
        lo = j * Q
        span = slice(lo, lo + Q)
        t = lo + lax.broadcasted_iota(jnp.int32, (Q, Q), 0)
        s = lo + lax.broadcasted_iota(jnp.int32, (Q, Q), 1)
        out_map = c_ref[span]
        scores = lax.dot_general(out_map, b_ref[span], (((1,), (1,)), ((), ())), preferred_element_type=F32)
        scores = jnp.where((s <= t) & (segment(t, ends) == segment(s, ends)), scores, 0.0)
        a, b = a_ref[0, span], bt_ref[:, span]
        if j:
            base = dot(lead[span], R) * dot(out_map, eloc[j - 1])
        for p in range(PER // 2):
            col = slice(2 * p * WIDTH, 2 * (p + 1) * WIDTH)
            m = [
                (jnp.exp2(jnp.minimum(a[:, h : h + 1] - b[h : h + 1, :], 60.0)) * scores).astype(BF)
                for h in (2 * p, 2 * p + 1)
            ]
            x = x_ref[span, col]
            y = dot(jnp.concatenate(m, axis=1), jnp.concatenate([x * low, x * high], axis=0))
            y = y + gain[:, col] * x.astype(F32)
            out[span, col] = y + base[:, col] if j else y


def local(lengths, me, xm, bm, cm, a2, b2, lead, eloc, small):
    T = xm.shape[0]
    n = T // Q
    return pl.pallas_call(
        functools.partial(local_kernel, n + 2 * SEQS + 1),
        grid=(GROUPS,),
        in_specs=[
            SMEM,
            SMEM,
            pl.BlockSpec((T, GW), lambda g: (0, g)),
            pl.BlockSpec((T, STATE), lambda g: (0, g)),
            pl.BlockSpec((T, STATE), lambda g: (0, g)),
            pl.BlockSpec((1, T, PER), lambda g: (g, 0, 0)),
            pl.BlockSpec((PER, T), lambda g: (g, 0)),
            pl.BlockSpec((T, 2 * HEADS), lambda g: (0, 0)),
            pl.BlockSpec((n - 1, STATE, GW), lambda g: (0, 0, g)),
            pl.BlockSpec(small.shape, lambda g: (0, 0)),
        ],
        out_specs=pl.BlockSpec((T, GW), lambda g: (0, g)),
        out_shape=jax.ShapeDtypeStruct((T, INNER), F32),
        compiler_params=params(),
        cost_estimate=pl.CostEstimate(flops=8 * 10**9, bytes_accessed=2 * 10**7, transcendentals=5 * 10**6),
        name="local",
    )(lengths, me, xm, bm, cm, a2, b2, lead, eloc, small)


def scan_kernel(T, lengths, me, got, enter, base, mail, value, ent):
    seqs, _, shard_w = got.shape
    _, _, share = mail.shape
    ends = stops(lengths, me, T)
    R = spread(me[0] * (shard_w // WIDTH), shard_w)
    ent[...] = jnp.zeros_like(ent)
    mail[...] = jnp.zeros_like(mail)
    for i in range(seqs):
        now = ent[...]
        enter[i] = now.astype(BF)
        state = got[i, 0:STATE].astype(F32)
        extra = got[i, STATE:]
        carry = dot(extra[:, 0:128], R)[3 * SEQS : 3 * SEQS + 1]
        for r in range(SEQS):
            stop = ends[r] + (me[0] - i) * T

            @pl.when((stop > 0) & (stop <= T))
            def _(r=r, now=now, state=state, extra=extra, stop=stop):
                at = slice(2 * SEQS + r, 2 * SEQS + r + 1)
                lead = dot(extra[:, 128:256], R)[at]
                base[r] = lead * now + jnp.where(stop == T, state, 0.0)
                hi, lo = halves(now)
                inter = (dot(extra[:, 0:128], hi) + dot(extra[:, 0:128], lo))[at]
                rows = extra.astype(F32)
                value[r : r + 1, :] = (rows[r : r + 1] + lead * inter) * silu(rows[SEQS + r : SEQS + r + 1])

        ent[...] = carry * now + state
    parts = shard_w // share
    v = value[0:SEQS]
    squares = jnp.broadcast_to(jnp.sum(v * v, axis=1, keepdims=True), (SEQS, share))
    for k in range(mail.shape[0]):
        mail[k, SEQS:] = squares
    for k in range(parts):
        mail[me[0] * parts + k, 0:SEQS] = value[0:SEQS, k * share : (k + 1) * share]


def scan(lengths, me, T, got, devices, share):
    seqs, _, shard_w = got.shape
    sds = jax.ShapeDtypeStruct
    return pl.pallas_call(
        functools.partial(scan_kernel, T),
        in_specs=[SMEM, SMEM, VMEM],
        out_specs=[VMEM] * 3,
        out_shape=[
            sds((seqs, STATE, shard_w), BF),
            sds((SEQS, STATE, shard_w), F32),
            sds((devices, 2 * SEQS, share), F32),
        ],
        scratch_shapes=[pltpu.VMEM((8, shard_w), F32), pltpu.VMEM((STATE, shard_w), F32)],
        compiler_params=params(),
        name="scan",
    )(lengths, me, got)


def finals_kernel(T, lengths, me, base, *refs):
    out = refs[-1]
    count = len(refs) - 1
    ends = stops(lengths, me, T)
    for r in range(SEQS):
        out[r] = base[r].T
        if r == SEQS - 1:
            continue
        last = ends[r] + me[0] * T - 1
        for c in range(count):

            @pl.when((last % T != T - 1) & ((last // (2 * T)) ^ (me[0] // 2) == c))
            def _(r=r, c=c):
                out[r] = (base[r] + refs[c][r % 2].astype(F32)).T


def finals(lengths, me, T, base, pieces):
    _, _, shard_w = base.shape
    return pl.pallas_call(
        functools.partial(finals_kernel, T),
        in_specs=[SMEM, SMEM] + [VMEM] * (1 + len(pieces)),
        out_specs=VMEM,
        out_shape=jax.ShapeDtypeStruct((SEQS, shard_w, STATE), F32),
        compiler_params=params(),
        name="finals",
    )(lengths, me, base, *pieces)


def finish_kernel(y_ref, gate, c_ref, e_ref, lead, norm, out):
    R = spread(pl.program_id(0) * PER, GW)
    entering = jnp.concatenate([e_ref[k] for k in range(e_ref.shape[0])], axis=1)
    y = y_ref[...] + dot(lead[...], R) * dot(c_ref[...], entering)
    v = y * silu(gate[...].astype(F32))
    scale = lax.rsqrt(jnp.sum(v * v, axis=1, keepdims=True) * (1.0 / GW) + TINY_FLOOR)
    out[...] = (v * scale * norm[...]).astype(BF)


def finish(y_local, gate, cm, enter, lead, norm):
    T = y_local.shape[0]
    seqs, _, shard_w = enter.shape
    tile = T
    return pl.pallas_call(
        finish_kernel,
        grid=(GROUPS, T // tile),
        in_specs=[
            pl.BlockSpec((tile, GW), lambda g, i: (i, g)),
            pl.BlockSpec((tile, GW), lambda g, i: (i, g)),
            pl.BlockSpec((tile, STATE), lambda g, i: (i, g)),
            pl.BlockSpec((GW // shard_w, STATE, shard_w), lambda g, i: (g, 0, 0)),
            pl.BlockSpec((tile, 2 * HEADS), lambda g, i: (i, 0)),
            pl.BlockSpec((1, GW), lambda g, i: (0, g)),
        ],
        out_specs=pl.BlockSpec((tile, GW), lambda g, i: (i, g)),
        out_shape=jax.ShapeDtypeStruct((T, INNER), BF),
        compiler_params=params(),
        cost_estimate=pl.CostEstimate(flops=2 * 10**9, bytes_accessed=2 * 10**7, transcendentals=4 * 10**6),
        name="finish",
    )(y_local, gate, cm, enter, lead, norm)


def largest_kernel(h_ref, w_ref, out):
    logits = lax.dot_general(w_ref[...], h_ref[...], (((1,), (1,)), ((), ())), preferred_element_type=F32)
    top = jnp.max(logits, axis=0, keepdims=True)
    first = pl.program_id(0) == 0
    out[...] = jnp.where(first, top, jnp.maximum(top, out[...]))


def largest(normed, vocab_weight):
    count, depth = normed.shape
    height = 1024
    return pl.pallas_call(
        largest_kernel,
        grid=(vocab_weight.shape[0] // height,),
        in_specs=[
            pl.BlockSpec((count, depth), lambda i: (0, 0)),
            pl.BlockSpec((height, depth), lambda i: (i, 0)),
        ],
        out_specs=pl.BlockSpec((1, count), lambda i: (0, 0)),
        out_shape=jax.ShapeDtypeStruct((1, count), F32),
        compiler_params=params(),
        name="largest",
    )(normed, vocab_weight)


def swap(x, seqs, distance):
    return lax.ppermute(x, "seq", [(i, i ^ distance) for i in range(seqs)])


def exchange(x, axes):
    return lax.all_to_all(x, axes, 0, 0, tiled=True)


def body(
    conv_input,
    gate_projected,
    step_raw,
    step_bias,
    decay_log,
    head_direct_gain,
    conv_weight,
    convolution_bias,
    norm_weight,
    lengths,
    out_weight,
    residual_last,
    final_gain,
    vocab_weight,
):
    every = ("req", "seq")
    T = conv_input.shape[1]
    seqs, reqs = lax.axis_size("seq"), lax.axis_size("req")
    seq_place, req_place = lax.axis_index("seq"), lax.axis_index("req")
    devices = seqs * reqs
    flat = req_place * seqs + seq_place
    shard_w = INNER // seqs
    share = out_weight.shape[0]
    rows_total = reqs * SEQS
    rows = conv_input[0]

    edge = lax.ppermute(rows[T - (KERNEL - 1) :], "seq", [(i, i + 1) for i in range(seqs - 1)])
    halo = jnp.pad(edge, ((16 - (KERNEL - 1), 0), (0, 0)))
    me = seq_place[None].astype(jnp.int32)
    lens = lengths[0].astype(jnp.int32)
    a2, b2, wst, leadj, lead0, pick, small = prep(
        lens, me, step_raw[0].T, step_bias[None], decay_log[None], head_direct_gain[None]
    )
    xm, bm, cm, pay, eloc, *slots = front(
        lens, me, rows, halo, conv_weight, convolution_bias[None], wst, pick, small, gate_projected[0], seqs
    )
    got = exchange(pay, "seq")
    y_local = local(lens, me, xm, bm, cm, a2, b2, leadj, eloc, small)
    got, y_local = lax.optimization_barrier((got, y_local))
    enter, base, mail = scan(lens, me, T, got, devices, share)

    mail, slots = lax.optimization_barrier((mail, slots))
    given = [swap(slots[2], seqs, 1)]
    mail = exchange(mail, every)
    mail, given, kept = lax.optimization_barrier((mail, given, slots[3]))
    given.append(swap(kept, seqs, 1))
    mail = mail.reshape(reqs, seqs, 2 * SEQS, share)
    v = lax.dynamic_index_in_dim(mail[:, :, :SEQS], flat * share // shard_w, 1, keepdims=False)
    near = GW // shard_w
    squares = lax.dynamic_slice_in_dim(mail[:, :, SEQS:], flat * share // GW * near, near, 1).sum(axis=1)
    v = v * lax.rsqrt(squares * (1.0 / GW) + TINY_FLOOR)
    u = (v * lax.dynamic_slice_in_dim(norm_weight, flat * share, share)).astype(BF).reshape(rows_total, share)
    partial = jnp.dot(u, out_weight, preferred_element_type=F32)
    chunk = D // devices
    mail = exchange(partial.reshape(rows_total, devices, chunk).transpose(1, 0, 2), every)
    own = mail.sum(axis=0)
    residual = residual_last.reshape(rows_total, D)
    own = own + lax.dynamic_slice_in_dim(residual, flat * chunk, chunk, 1).astype(F32)
    mail = exchange(jnp.broadcast_to(own.astype(BF), (devices, rows_total, chunk)), every).astype(F32)
    hidden = mail.transpose(1, 0, 2).reshape(rows_total, D)
    hidden, enter = lax.optimization_barrier((hidden, enter))
    entering = exchange(enter, "seq")
    rms = lax.rsqrt(jnp.mean(hidden * hidden, axis=-1, keepdims=True) + TINY_FLOOR)
    normed = (hidden * rms * final_gain).astype(BF)
    last_hidden = lax.dynamic_slice_in_dim(hidden.reshape(reqs, SEQS, D), req_place, 1, 0).astype(BF)
    top = largest(normed, vocab_weight).reshape(reqs, 1, SEQS)
    top = jnp.broadcast_to(top, (reqs, seqs, SEQS)).reshape(devices, SEQS)
    top, entering, given = lax.optimization_barrier((top, entering, given))

    pair = seq_place // 2
    tails = [
        jnp.stack([
            lax.dynamic_index_in_dim(kept, pair ^ c, 0, keepdims=False) + lax.dynamic_index_in_dim(other, pair ^ c, 0, keepdims=False)
            for kept, other in zip(slots[:2], given)
        ])
        for c in range(seqs // 2)
    ]
    tails, entering = lax.optimization_barrier((tails, entering))
    tails = [tails[0]] + [swap(tails[c], seqs, 2 * c) for c in range(1, seqs // 2)]
    y_gated = finish(y_local, gate_projected[0], cm, entering, lead0, norm_weight[None])

    max_logit = jnp.max(exchange(top, every), axis=0, keepdims=True)
    final_states = finals(lens, me, T, base, tails).reshape(1, SEQS, HEADS // seqs, WIDTH, STATE)
    return (y_gated[None], final_states, last_hidden, max_logit)


def solution(mesh):
    return jax.shard_map(
        body,
        mesh=mesh,
        in_specs=(
            P("req", "seq", None),
            P("req", "seq", None),
            P("req", "seq", None),
            P(),
            P(),
            P(),
            P(),
            P(),
            P(),
            P("req", None),
            P(("req", "seq"), None),
            P(),
            P(),
            P(("req", "seq"), None),
        ),
        out_specs=(
            P("req", "seq", None),
            P("req", None, "seq", None, None),
            P("req", None, None),
            P("req", None),
        ),
        check_vma=False,
    )
```

```python
import functools
import math

import jax
import jax.numpy as jnp
from jax import lax
from jax.experimental import pallas as pl
from jax.experimental.pallas import tpu as pltpu
from jax.sharding import PartitionSpec as P

D = 4096
HEADS = 64
WIDTH = 64
GROUPS = 4
STATE = 128
KERNEL = 4
SEQS = 4
INNER = HEADS * WIDTH
PER = HEADS // GROUPS
GW = INNER // GROUPS
Q = 128
EXTRA = 16
TINY_FLOOR = 1e-05
LOG2E = 1.0 / math.log(2.0)
BF = jnp.bfloat16
F32 = jnp.float32
HI = lax.Precision.HIGHEST


def params(mib):
    return pltpu.CompilerParams(vmem_limit_bytes=mib * 1024 * 1024)


def dot(a, b):
    return jnp.dot(a, b, preferred_element_type=F32)


def halves(x):
    hi = x.astype(BF)
    return hi, (x - hi.astype(F32)).astype(BF)


def spread(first_head, width):
    head = lax.broadcasted_iota(jnp.int32, (2 * HEADS, width), 0) % HEADS
    channel = lax.broadcasted_iota(jnp.int32, (2 * HEADS, width), 1)
    return (head == first_head + channel // WIDTH).astype(F32).astype(BF)


def silu(x):
    half = 0.5 * x
    return half + half * jnp.tanh(half)


def stops(lengths, me, T):
    total, ends = -me[0] * T, []
    for k in range(SEQS):
        total = total + lengths[k]
        ends.append(total)
    return ends


def segment(place, ends):
    return sum([(place >= ends[k]).astype(jnp.int32) for k in range(SEQS - 1)])


def prep_kernel(lengths, me, raw_ref, bias_ref, log_ref, gain_ref, a_ref, b_ref, wst_ref, leadj_ref, lead0_ref, pick_ref, small_ref, cum, lj, l0, rows):
    T = raw_ref.shape[1]
    ends = stops(lengths, me, T)
    z = raw_ref[...] + jnp.broadcast_to(bias_ref[...], (8, HEADS)).T[:, 0:1]
    u = jnp.exp(-jnp.abs(z))
    series = u * (1.0 - u * (0.5 - u * (1.0 / 3.0 - u * (0.25 - u * 0.2))))
    dt_t = jnp.maximum(z, 0.0) + jnp.where(u < 0.03, series, jnp.log(1.0 + u))
    dec = -jnp.exp(jnp.broadcast_to(log_ref[...], (8, HEADS)).T[:, 0:1]) * dt_t
    earlier = lax.broadcasted_iota(jnp.int32, (T, T), 0)
    later = lax.broadcasted_iota(jnp.int32, (T, T), 1)
    total_t = jnp.dot(dec, (later >= earlier).astype(F32), precision=HI, preferred_element_type=F32)
    b_ref[...] = (total_t - jnp.log(dt_t)) * LOG2E
    total, dt = total_t.T, dt_t.T
    cum[...] = total
    a2 = total * LOG2E
    for g in range(GROUPS):
        a_ref[g] = a2[:, g * PER : (g + 1) * PER]
    place = lax.broadcasted_iota(jnp.int32, (T, HEADS), 0)
    seg = segment(place, ends)
    lead0 = jnp.where(seg == segment(-1, ends), jnp.exp(total), 0.0)
    l0[...] = lead0
    target = lax.broadcasted_iota(jnp.int32, (Q, Q + 16), 0)
    source = lax.broadcasted_iota(jnp.int32, (Q, Q + 16), 1) - 16
    for j in range(T // Q):
        same = segment(j * Q + target, ends) == segment(j * Q + source, ends)
        for k in range(KERNEL - 1):
            chosen = same & (source == target + (k - (KERNEL - 1)))
            pick_ref[j, k * Q : (k + 1) * Q] = chosen.astype(F32).astype(BF)
    at_stop = [cum[pl.ds(jnp.clip(ends[r] - 1, 0, T - 1), 1), :] for r in range(SEQS)]
    for j in range(T // Q):
        lo, hi = j * Q, (j + 1) * Q
        part = total[lo:hi]
        aim = jnp.broadcast_to(total[hi - 1 : hi], (Q, HEADS))
        for r in range(SEQS - 1):
            aim = jnp.where((seg[lo:hi] == r) & (ends[r] < hi), at_stop[r], aim)
        weight = jnp.exp(aim - part) * dt[lo:hi]
        wst_ref[lo:hi] = jnp.concatenate(halves(weight), axis=1)
        base = total[lo - 1 : lo] if j else 0.0
        lead = jnp.where(seg[lo:hi] == segment(lo - 1, ends), jnp.exp(part - base), 0.0)
        lj[lo:hi] = lead
        rows[j : j + 1] = lead[Q - 1 :]
    leadj_ref[...] = jnp.concatenate(halves(lj[...]), axis=1)
    lead0_ref[...] = jnp.concatenate(halves(lead0), axis=1)
    n = T // Q
    for r in range(SEQS):
        stop = ends[r] - 1
        owned = ((stop >= 0) & (stop < T)).astype(F32)
        at = pl.ds(jnp.clip(stop, 0, T - 1), 1)
        rows[n + r : n + r + 1] = lj[at, :] * owned
        rows[n + SEQS + r : n + SEQS + r + 1] = l0[at, :] * owned
    rows[n + 2 * SEQS : n + 2 * SEQS + 1] = lead0[T - 1 :]
    rows[n + 2 * SEQS + 1 : n + 2 * SEQS + 2] = gain_ref[...]
    small_ref[...] = jnp.concatenate(halves(rows[...]), axis=1)


SMEM = pl.BlockSpec(memory_space=pltpu.SMEM)
VMEM = pl.BlockSpec(memory_space=pltpu.VMEM)


def prep(lengths, me, raw, bias, decay_log, gain):
    T = raw.shape[1]
    nrows = -(-(T // Q + 2 * SEQS + 2) // 16) * 16
    sds = jax.ShapeDtypeStruct
    return pl.pallas_call(
        prep_kernel,
        in_specs=[SMEM, SMEM] + [VMEM] * 4,
        out_specs=[VMEM] * 7,
        out_shape=[
            sds((GROUPS, T, PER), F32),
            sds((HEADS, T), F32),
            sds((T, 2 * HEADS), BF),
            sds((T, 2 * HEADS), BF),
            sds((T, 2 * HEADS), BF),
            sds((T // Q, (KERNEL - 1) * Q, Q + 16), BF),
            sds((nrows, 2 * HEADS), BF),
        ],
        scratch_shapes=[
            pltpu.VMEM((T, HEADS), F32),
            pltpu.VMEM((T, HEADS), F32),
            pltpu.VMEM((T, HEADS), F32),
            pltpu.VMEM((nrows, HEADS), F32),
        ],
        compiler_params=params(56),
        name="prep",
    )(lengths, me, raw, bias, decay_log, gain)


def front_kernel(seqs, shard_w, lengths, me, x_ref, b_ref, c_ref, hx, hb, hc, wx, wb, wc, bx, bb, bc, wst, pick, small, gate,
                 xm, bm, cm, pay, eloc, keep0, keep1, give0, give1, act, ent, exs, near, sems):
    slots = ((keep0, keep1), (give0, give1))
    T = x_ref.shape[0]
    n = T // Q
    g = pl.program_id(0)
    ends = stops(lengths, me, T)
    span = me[0]
    shards = GW // shard_w
    cuts = [slice(k * shard_w, (k + 1) * shard_w) for k in range(shards)]
    R = spread(g * PER, GW)
    wide = dot(small[...], R)
    packed = small[...].astype(F32)
    gain = wide[n + 2 * SEQS + 1 : n + 2 * SEQS + 2]
    pieces = [
        (x_ref, hx, wx, bx, xm, 0, GW),
        (b_ref, hb, wb, bb, bm, GW, STATE),
        (c_ref, hc, wc, bc, cm, GW + STATE, STATE),
    ]
    spots = [jnp.clip(ends[r] - 1, 0, T - 1) for r in range(SEQS)]

    def fetch(r):
        top = pl.multiple_of(spots[r] // 16 * 16, 16)
        cols = pl.ds(pl.multiple_of(g * GW, GW), GW)
        return pltpu.make_async_copy(gate.at[pl.ds(top, 16), cols], near.at[r], sems.at[r])

    for r in range(SEQS):
        fetch(r).start()
    ent[...] = jnp.zeros_like(ent)
    for slot in slots[0] + slots[1]:
        slot[...] = jnp.zeros_like(slot)
    exs[...] = jnp.zeros_like(exs)
    for k in range(shards):
        exs[k, 3 * SEQS : 3 * SEQS + 1, 0:128] = packed[n + 2 * SEQS : n + 2 * SEQS + 1]

    for j in range(n):
        lo = j * Q
        for src, halo, w_ref, bias, out, at, w in pieces:
            own = src[lo : lo + Q]
            window = jnp.concatenate([src[lo - 16 : lo] if j else halo[...], own], axis=0)
            for c in range(0, w, 512):
                c2 = min(c + 512, w)
                near3 = dot(pick[j], window[:, c:c2])
                acc = bias[:, c:c2] + w_ref[KERNEL - 1 : KERNEL, c:c2] * own[:, c:c2].astype(F32)
                for k in range(KERNEL - 1):
                    acc = acc + w_ref[k : k + 1, c:c2] * near3[k * Q : (k + 1) * Q]
                y = silu(acc)
                act[lo : lo + Q, at + c : at + c2] = y
                out[lo : lo + Q, c:c2] = y.astype(BF)
        scaled = act[lo : lo + Q, :GW] * dot(wst[lo : lo + Q], R)
        xhi, xlo = halves(scaled)
        right = jnp.concatenate([xhi, xlo], axis=0)
        bt = act[lo : lo + Q, GW : GW + STATE].T
        lane_seg = segment(lo + lax.broadcasted_iota(jnp.int32, (STATE, Q), 1), ends)

        def gathered(which, bt=bt, lane_seg=lane_seg, right=right):
            bhi = jnp.where(lane_seg == which, bt, 0.0).astype(BF)
            return dot(jnp.concatenate([bhi, bhi], axis=1), right)

        if j:
            eloc[j - 1] = ent[...].astype(BF)
        for r in range(SEQS):
            stop = ends[r] - 1

            @pl.when((stop >= lo) & (stop < lo + Q))
            def _(r=r, stop=stop, gathered=gathered):
                tail = wide[n + r : n + r + 1] * ent[...] + gathered(r)
                if r < SEQS - 1:
                    fits = stop < T - 1
                    if r != 1:
                        fits = fits & ((span < seqs // 2) if r == 0 else (span >= seqs // 2))
                    for p in range(2):

                        @pl.when(fits & (span % 2 == p))
                        def _(p=p):
                            for k in range(shards):
                                to = slots[0 if k % 2 == p else 1][r % 2]
                                to[k // 2] = tail[:, cuts[k]].astype(BF)

                row = act[pl.ds(stop, 1), :].astype(BF)
                out_map = jnp.broadcast_to(row[:, GW + STATE :], (16, STATE))
                thi, tlo = halves(tail)
                value = (dot(out_map, thi) + dot(out_map, tlo))[0:1]
                value = value + gain * row[:, :GW].astype(F32)
                for k in range(shards):
                    exs[k, r : r + 1, :] = value[:, cuts[k]]
                    exs[k, 2 * SEQS + r : 2 * SEQS + r + 1, 0:128] = row[:, GW + STATE :].astype(F32)
                    exs[k, 2 * SEQS + r : 2 * SEQS + r + 1, 128:256] = packed[n + SEQS + r : n + SEQS + r + 1]

        ent[...] = wide[j : j + 1] * ent[...] + gathered(segment(lo + Q - 1, ends))
    for r in range(SEQS):
        fetch(r).wait()
        mine = lax.broadcasted_iota(jnp.int32, (16, GW), 0) == spots[r] % 16
        owned = (spots[r] == ends[r] - 1).astype(F32)
        line = jnp.sum(jnp.where(mine, near[r].astype(F32), 0.0), axis=0, keepdims=True) * owned
        for k in range(shards):
            exs[k, SEQS + r : SEQS + r + 1, :] = line[:, cuts[k]]
    for k in range(shards):
        pay[k, 0:STATE, :] = ent[:, cuts[k]].astype(BF)
        pay[k, STATE:, :] = exs[k].astype(BF)


def front(lengths, me, rows, halo, conv_weight, bias, wst, pick, small, gate, seqs):
    T = rows.shape[0]
    shard_w = INNER // seqs
    shards = GW // shard_w
    n = T // Q
    first_b, first_c = INNER // STATE, INNER // STATE + GROUPS
    sds = jax.ShapeDtypeStruct

    def three(height):
        return [
            pl.BlockSpec((height, GW), lambda g: (0, g)),
            pl.BlockSpec((height, STATE), lambda g: (0, first_b + g)),
            pl.BlockSpec((height, STATE), lambda g: (0, first_c + g)),
        ]

    whole = lambda a: pl.BlockSpec(a.shape, lambda g: (0, 0))
    return pl.pallas_call(
        functools.partial(front_kernel, seqs, shard_w),
        grid=(GROUPS,),
        in_specs=[SMEM, SMEM]
        + three(T)
        + three(16)
        + three(KERNEL)
        + three(1)
        + [whole(wst), pl.BlockSpec(pick.shape, lambda g: (0, 0, 0)), whole(small), pl.BlockSpec(memory_space=pl.ANY)],
        out_specs=[
            pl.BlockSpec((T, GW), lambda g: (0, g)),
            pl.BlockSpec((T, STATE), lambda g: (0, g)),
            pl.BlockSpec((T, STATE), lambda g: (0, g)),
            pl.BlockSpec((shards, STATE + EXTRA, shard_w), lambda g: (g, 0, 0)),
            pl.BlockSpec((n - 1, STATE, GW), lambda g: (0, 0, g)),
        ]
        + [pl.BlockSpec((shards // 2, STATE, shard_w), lambda g: (g, 0, 0))] * 4,
        out_shape=[
            sds((T, INNER), BF),
            sds((T, GROUPS * STATE), BF),
            sds((T, GROUPS * STATE), BF),
            sds((seqs, STATE + EXTRA, shard_w), BF),
            sds((n - 1, STATE, INNER), BF),
        ]
        + [sds((seqs // 2, STATE, shard_w), BF)] * 4,
        scratch_shapes=[
            pltpu.VMEM((T, GW + 2 * STATE), F32),
            pltpu.VMEM((STATE, GW), F32),
            pltpu.VMEM((shards, EXTRA, shard_w), F32),
            pltpu.VMEM((SEQS, 16, GW), BF),
            pltpu.SemaphoreType.DMA((SEQS,)),
        ],
        compiler_params=params(56),
        name="front",
    )(lengths, me, rows, rows, rows, halo, halo, halo, conv_weight, conv_weight, conv_weight, bias, bias, bias, wst, pick, small, gate)


def local_kernel(gain_row, lengths, me, x_ref, b_ref, c_ref, a_ref, bt_ref, lead, eloc, small, out):
    T = x_ref.shape[0]
    ends = stops(lengths, me, T)
    R = spread(pl.program_id(0) * PER, GW)
    wide = dot(small[...], R)
    gain = wide[gain_row : gain_row + 1]
    low = (lax.broadcasted_iota(jnp.int32, (Q, 2 * WIDTH), 1) < WIDTH).astype(F32).astype(BF)
    high = 1 - low
    for j in range(T // Q):
        lo = j * Q
        span = slice(lo, lo + Q)
        t = lo + lax.broadcasted_iota(jnp.int32, (Q, Q), 0)
        s = lo + lax.broadcasted_iota(jnp.int32, (Q, Q), 1)
        out_map = c_ref[span]
        scores = lax.dot_general(out_map, b_ref[span], (((1,), (1,)), ((), ())), preferred_element_type=F32)
        scores = jnp.where((s <= t) & (segment(t, ends) == segment(s, ends)), scores, 0.0)
        a, b = a_ref[0, span], bt_ref[:, span]
        if j:
            base = dot(lead[span], R) * dot(out_map, eloc[j - 1])
        for p in range(PER // 2):
            col = slice(2 * p * WIDTH, 2 * (p + 1) * WIDTH)
            m = [
                (jnp.exp2(jnp.minimum(a[:, h : h + 1] - b[h : h + 1, :], 60.0)) * scores).astype(BF)
                for h in (2 * p, 2 * p + 1)
            ]
            x = x_ref[span, col]
            y = dot(jnp.concatenate(m, axis=1), jnp.concatenate([x * low, x * high], axis=0))
            y = y + gain[:, col] * x.astype(F32)
            out[span, col] = y + base[:, col] if j else y


def local(lengths, me, xm, bm, cm, a2, b2, lead, eloc, small):
    T = xm.shape[0]
    n = T // Q
    return pl.pallas_call(
        functools.partial(local_kernel, n + 2 * SEQS + 1),
        grid=(GROUPS,),
        in_specs=[
            SMEM,
            SMEM,
            pl.BlockSpec((T, GW), lambda g: (0, g)),
            pl.BlockSpec((T, STATE), lambda g: (0, g)),
            pl.BlockSpec((T, STATE), lambda g: (0, g)),
            pl.BlockSpec((1, T, PER), lambda g: (g, 0, 0)),
            pl.BlockSpec((PER, T), lambda g: (g, 0)),
            pl.BlockSpec((T, 2 * HEADS), lambda g: (0, 0)),
            pl.BlockSpec((n - 1, STATE, GW), lambda g: (0, 0, g)),
            pl.BlockSpec(small.shape, lambda g: (0, 0)),
        ],
        out_specs=pl.BlockSpec((T, GW), lambda g: (0, g)),
        out_shape=jax.ShapeDtypeStruct((T, INNER), F32),
        compiler_params=params(56),
        cost_estimate=pl.CostEstimate(flops=8 * 10**9, bytes_accessed=2 * 10**7, transcendentals=5 * 10**6),
        name="local",
    )(lengths, me, xm, bm, cm, a2, b2, lead, eloc, small)


def scan_kernel(T, lengths, me, got, enter, base, mail, value, ent):
    seqs, _, shard_w = got.shape
    _, _, share = mail.shape
    ends = stops(lengths, me, T)
    R = spread(me[0] * (shard_w // WIDTH), shard_w)
    ent[...] = jnp.zeros_like(ent)
    mail[...] = jnp.zeros_like(mail)
    for i in range(seqs):
        now = ent[...]
        enter[i] = now.astype(BF)
        state = got[i, 0:STATE].astype(F32)
        extra = got[i, STATE:]
        carry = dot(extra[:, 0:128], R)[3 * SEQS : 3 * SEQS + 1]
        for r in range(SEQS):
            stop = ends[r] + (me[0] - i) * T

            @pl.when((stop > 0) & (stop <= T))
            def _(r=r, now=now, state=state, extra=extra, stop=stop):
                at = slice(2 * SEQS + r, 2 * SEQS + r + 1)
                lead = dot(extra[:, 128:256], R)[at]
                base[r] = lead * now + jnp.where(stop == T, state, 0.0)
                hi, lo = halves(now)
                inter = (dot(extra[:, 0:128], hi) + dot(extra[:, 0:128], lo))[at]
                rows = extra.astype(F32)
                value[r : r + 1, :] = (rows[r : r + 1] + lead * inter) * silu(rows[SEQS + r : SEQS + r + 1])

        ent[...] = carry * now + state
    parts = shard_w // share
    v = value[0:SEQS]
    squares = jnp.broadcast_to(jnp.sum(v * v, axis=1, keepdims=True), (SEQS, share))
    for k in range(mail.shape[0]):
        mail[k, SEQS:] = squares
    for k in range(parts):
        mail[me[0] * parts + k, 0:SEQS] = value[0:SEQS, k * share : (k + 1) * share]


def scan(lengths, me, T, got, devices, share):
    seqs, _, shard_w = got.shape
    sds = jax.ShapeDtypeStruct
    return pl.pallas_call(
        functools.partial(scan_kernel, T),
        in_specs=[SMEM, SMEM, VMEM],
        out_specs=[VMEM] * 3,
        out_shape=[
            sds((seqs, STATE, shard_w), BF),
            sds((SEQS, STATE, shard_w), F32),
            sds((devices, 2 * SEQS, share), F32),
        ],
        scratch_shapes=[pltpu.VMEM((8, shard_w), F32), pltpu.VMEM((STATE, shard_w), F32)],
        compiler_params=params(8),
        name="scan",
    )(lengths, me, got)


def finals_kernel(T, lengths, me, base, *refs):
    out = refs[-1]
    count = len(refs) - 1
    ends = stops(lengths, me, T)
    for r in range(SEQS):
        out[r] = base[r].T
        if r == SEQS - 1:
            continue
        last = ends[r] + me[0] * T - 1
        for c in range(count):

            @pl.when((last % T != T - 1) & ((last // (2 * T)) ^ (me[0] // 2) == c))
            def _(r=r, c=c):
                out[r] = (base[r] + refs[c][r % 2].astype(F32)).T


def finals(lengths, me, T, base, pieces):
    _, _, shard_w = base.shape
    return pl.pallas_call(
        functools.partial(finals_kernel, T),
        in_specs=[SMEM, SMEM] + [VMEM] * (1 + len(pieces)),
        out_specs=VMEM,
        out_shape=jax.ShapeDtypeStruct((SEQS, shard_w, STATE), F32),
        compiler_params=params(56),
        name="finals",
    )(lengths, me, base, *pieces)


def finish_kernel(y_ref, gate, c_ref, e_ref, lead, norm, out):
    R = spread(pl.program_id(0) * PER, GW)
    entering = jnp.concatenate([e_ref[k] for k in range(e_ref.shape[0])], axis=1)
    y = y_ref[...] + dot(lead[...], R) * dot(c_ref[...], entering)
    v = y * silu(gate[...].astype(F32))
    scale = lax.rsqrt(jnp.sum(v * v, axis=1, keepdims=True) * (1.0 / GW) + TINY_FLOOR)
    out[...] = (v * scale * norm[...]).astype(BF)


def finish(y_local, gate, cm, enter, lead, norm):
    T = y_local.shape[0]
    seqs, _, shard_w = enter.shape
    tile = T
    return pl.pallas_call(
        finish_kernel,
        grid=(GROUPS, T // tile),
        in_specs=[
            pl.BlockSpec((tile, GW), lambda g, i: (i, g)),
            pl.BlockSpec((tile, GW), lambda g, i: (i, g)),
            pl.BlockSpec((tile, STATE), lambda g, i: (i, g)),
            pl.BlockSpec((GW // shard_w, STATE, shard_w), lambda g, i: (g, 0, 0)),
            pl.BlockSpec((tile, 2 * HEADS), lambda g, i: (i, 0)),
            pl.BlockSpec((1, GW), lambda g, i: (0, g)),
        ],
        out_specs=pl.BlockSpec((tile, GW), lambda g, i: (i, g)),
        out_shape=jax.ShapeDtypeStruct((T, INNER), BF),
        compiler_params=params(56),
        cost_estimate=pl.CostEstimate(flops=2 * 10**9, bytes_accessed=2 * 10**7, transcendentals=4 * 10**6),
        name="finish",
    )(y_local, gate, cm, enter, lead, norm)


def largest_kernel(h_ref, w_ref, mail, out):
    logits = lax.dot_general(w_ref[...], h_ref[...], (((1,), (1,)), ((), ())), preferred_element_type=F32)
    top = jnp.max(logits, axis=0, keepdims=True)
    first = pl.program_id(0) == 0
    out[...] = jnp.where(first, top, jnp.maximum(top, out[...]))

    @pl.when(pl.program_id(0) == pl.num_programs(0) - 1)
    def _():
        reqs = out.shape[1] // SEQS
        seqs = mail.shape[0] // reqs
        for b in range(reqs):
            mail[b * seqs : (b + 1) * seqs] = jnp.broadcast_to(out[:, b * SEQS : (b + 1) * SEQS], (seqs, SEQS))


def largest(normed, vocab_weight, devices):
    count, depth = normed.shape
    height = 1024
    return pl.pallas_call(
        largest_kernel,
        grid=(vocab_weight.shape[0] // height,),
        in_specs=[
            pl.BlockSpec((count, depth), lambda i: (0, 0)),
            pl.BlockSpec((height, depth), lambda i: (i, 0)),
        ],
        out_specs=pl.BlockSpec((devices, SEQS), lambda i: (0, 0)),
        out_shape=jax.ShapeDtypeStruct((devices, SEQS), F32),
        scratch_shapes=[pltpu.VMEM((1, count), F32)],
        compiler_params=params(56),
        name="largest",
    )(normed, vocab_weight)


def swap(x, seqs, distance):
    return lax.ppermute(x, "seq", [(i, i ^ distance) for i in range(seqs)])


def exchange(x, axes):
    return lax.all_to_all(x, axes, 0, 0, tiled=True)


def body(
    conv_input,
    gate_projected,
    step_raw,
    step_bias,
    decay_log,
    head_direct_gain,
    conv_weight,
    convolution_bias,
    norm_weight,
    lengths,
    out_weight,
    residual_last,
    final_gain,
    vocab_weight,
):
    every = ("req", "seq")
    T = conv_input.shape[1]
    seqs, reqs = lax.axis_size("seq"), lax.axis_size("req")
    seq_place, req_place = lax.axis_index("seq"), lax.axis_index("req")
    devices = seqs * reqs
    flat = req_place * seqs + seq_place
    shard_w = INNER // seqs
    share = out_weight.shape[0]
    rows_total = reqs * SEQS
    rows = conv_input[0]

    halo = lax.ppermute(rows[T - 16 :], "seq", [(i, i + 1) for i in range(seqs - 1)])
    me = seq_place[None].astype(jnp.int32)
    lens = lengths[0].astype(jnp.int32)
    a2, b2, wst, leadj, lead0, pick, small = prep(
        lens, me, step_raw[0].T, step_bias[None], decay_log[None], head_direct_gain[None]
    )
    xm, bm, cm, pay, eloc, *slots = front(
        lens, me, rows, halo, conv_weight, convolution_bias[None], wst, pick, small, gate_projected[0], seqs
    )
    got = exchange(pay, "seq")
    y_local = local(lens, me, xm, bm, cm, a2, b2, leadj, eloc, small)
    given = [swap(slots[2], seqs, 1)]
    got, y_local, given = lax.optimization_barrier((got, y_local, given))
    enter, base, mail = scan(lens, me, T, got, devices, share)

    mail, slots = lax.optimization_barrier((mail, slots))
    given.append(swap(slots[3], seqs, 1))
    mail = exchange(mail, every)
    mail, given = lax.optimization_barrier((mail, given))
    mail = mail.reshape(reqs, seqs, 2 * SEQS, share)
    pair = seq_place // 2

    def tail(c):
        return jnp.stack([
            lax.dynamic_index_in_dim(kept, pair ^ c, 0, keepdims=False) + lax.dynamic_index_in_dim(other, pair ^ c, 0, keepdims=False)
            for kept, other in zip(slots[:2], given)
        ])

    v = lax.dynamic_index_in_dim(mail[:, :, :SEQS], flat * share // shard_w, 1, keepdims=False)
    near = GW // shard_w
    squares = lax.dynamic_slice_in_dim(mail[:, :, SEQS:], flat * share // GW * near, near, 1).sum(axis=1)
    v = v * lax.rsqrt(squares * (1.0 / GW) + TINY_FLOOR)
    u = (v * lax.dynamic_slice_in_dim(norm_weight, flat * share, share)).astype(BF).reshape(rows_total, share)
    partial = jnp.dot(u, out_weight, preferred_element_type=F32)
    chunk = D // devices
    early = [seqs // 4]
    tails = {c: swap(tail(c), seqs, 2 * c) for c in early}
    mail = exchange(partial.reshape(rows_total, devices, chunk).transpose(1, 0, 2), every)
    mail, tails = lax.optimization_barrier((mail, tails))
    own = mail.sum(axis=0)
    residual = residual_last.reshape(rows_total, D)
    own = own + lax.dynamic_slice_in_dim(residual, flat * chunk, chunk, 1).astype(F32)
    mail = exchange(jnp.broadcast_to(own.astype(BF), (devices, rows_total, chunk)), every).astype(F32)
    hidden = mail.transpose(1, 0, 2).reshape(rows_total, D)
    hidden, enter, tails = lax.optimization_barrier((hidden, enter, tails))
    entering = exchange(enter, "seq")
    rms = lax.rsqrt(jnp.mean(hidden * hidden, axis=-1, keepdims=True) + TINY_FLOOR)
    normed = (hidden * rms * final_gain).astype(BF)
    last_hidden = lax.dynamic_slice_in_dim(hidden.reshape(reqs, SEQS, D), req_place, 1, 0).astype(BF)
    top = largest(normed, vocab_weight, devices)
    top, entering = lax.optimization_barrier((top, entering))

    late = [c for c in range(seqs // 2) if c not in early]
    rest, entering = lax.optimization_barrier(([tail(c) for c in late], entering))
    for c, x in zip(late, rest):
        tails[c] = swap(x, seqs, 2 * c) if c else x
    tails = [tails[c] for c in range(seqs // 2)]
    y_gated = finish(y_local, gate_projected[0], cm, entering, lead0, norm_weight[None])

    max_logit = jnp.max(exchange(top, every), axis=0, keepdims=True)
    final_states = finals(lens, me, T, base, tails).reshape(1, SEQS, HEADS // seqs, WIDTH, STATE)
    return (y_gated[None], final_states, last_hidden, max_logit)


def solution(mesh):
    return jax.shard_map(
        body,
        mesh=mesh,
        in_specs=(
            P("req", "seq", None),
            P("req", "seq", None),
            P("req", "seq", None),
            P(),
            P(),
            P(),
            P(),
            P(),
            P(),
            P("req", None),
            P(("req", "seq"), None),
            P(),
            P(),
            P(("req", "seq"), None),
        ),
        out_specs=(
            P("req", "seq", None),
            P("req", None, "seq", None, None),
            P("req", None, None),
            P("req", None),
        ),
        check_vma=False,
    )
```
